512 devices in a mesh: feature: 8 (over y_lo, x), latent: 64 (over z, y_hi, core).
Axes of the slice: x: 4, y: 4 (y_hi: 2, y_lo: 2; y = y_hi * 2 + y_lo), z: 16, core: 2. Of those that a mesh axis runs over, the one named last changes fastest.
Arguments:
- activations: bfloat16 [320, 2, 8192], P('latent', None, 'feature'), may hold values from -6 to 6
- targets: bfloat16 [320, 2, 8192], P('latent', None, 'feature'), may hold values from -6 to 6
- enc_weight: bfloat16 [2, 8192, 16384], P(None, 'feature', 'latent'), may hold values from -0.0625 to 0.0625
- enc_bias: float32 [2, 16384], P(None, 'latent'), may hold values from -5 to 5
- dec_weight: bfloat16 [3, 16384, 8192], P(None, 'latent', 'feature'), may hold values from -0.09375 to 0.09375
- top_blocks: int32 [320, 2, 16], replicated, may hold values from 0 to 127, as said below
- pair_mask: int32 [2, 2, 128], replicated, may hold values from 0 to 1, as said below
Outputs:
- recon: bfloat16 [320, 2, 8192], P('latent', None, 'feature')
- enc_grad: float32 [2, 8192, 16384], P(None, 'feature', 'latent')
The draws below stay inside these ranges and needn't reach their ends.
Inputs may be any that keep to these rules, and one draw needn't show every extreme that they name: `top_blocks`: for each row and layer the 16 block numbers are distinct. pair_mask[s, t, b] is 1 where s equals t and 0 where s is after t.
All inputs are finite; a program needn't handle non-finite values.
Results may differ from the reference program's by a relative error of at most 0.0051.
Values may be sent and summed in bfloat16 or wider, within the bound.
A program may use at most 64 MiB of HBM per device.

```python
import math
import jax
import jax.numpy as jnp
from jax import lax

D = 8192
F = 16384
BLOCK = 128
K = 16
LAYERS = 2
ROWS = 320
PAIRS = 3


def draw_top_blocks(key, part):
    key = jax.random.fold_in(key, 11)
    key_favour, key_jitter = jax.random.split(key)
    block_count = F // BLOCK
    favour = jax.random.randint(key_favour, (block_count,), 0, 2) * 2 ** 17
    jitter = jax.random.randint(key_jitter, (ROWS, LAYERS, block_count), 0, 2 ** 18)
    scores = (favour + jitter) * block_count + jnp.arange(block_count, dtype=jnp.int32)
    return lax.top_k(scores, K)[1].astype(jnp.int32)


def draw_pair_mask(key, part):
    key = jax.random.fold_in(key, 23)
    block_count = F // BLOCK
    coin_flips = jax.random.randint(key, (LAYERS, LAYERS, block_count), 0, 2)
    source = jnp.arange(LAYERS, dtype=jnp.int32)[:, None, None]
    later = jnp.arange(LAYERS, dtype=jnp.int32)[None, :, None]
    upper = jnp.where(source < later, coin_flips, jnp.zeros_like(coin_flips))
    return jnp.where(source == later, jnp.ones_like(coin_flips), upper).astype(jnp.int32)


def shard_levels(rng, dims, cuts, least, high):
    gain, own = 1.0, jax.random.fold_in(rng, 6)
    for position, shards_of in cuts:
        heights = jnp.exp(jax.random.uniform(jax.random.fold_in(own, position), (shards_of,), jnp.float32, least / len(cuts), high / len(cuts)))
        gain = gain * jnp.repeat(heights, dims[position] // shards_of).reshape([-1 if axis == position else 1 for axis in range(len(dims))])
    return gain


def bell_draw(key, extent, spread, limit, cuts=(), kind=jnp.bfloat16):
    result = jax.random.normal(key, extent, jnp.float32) * spread
    if len(cuts) > 0:
        result = shard_levels(key, extent, cuts, -0.22, 0.18) * result
    return jnp.clip(result, min=-limit, max=limit).astype(kind)


def setup_inputs(seed: int = 0) -> dict:
    splits = jax.random.split(jax.random.key(seed), 8)
    activations = bell_draw(splits[0], (ROWS, LAYERS, D), 1.0, 6.0, ((0, 64), (2, 8)))
    targets = bell_draw(splits[1], (ROWS, LAYERS, D), 1.0, 6.0, ((0, 64), (2, 8)))
    enc_weight = bell_draw(splits[2], (LAYERS, D, F), D ** -0.5, 0.0625, ((1, 8), (2, 64)))
    enc_bias = bell_draw(splits[3], (LAYERS, F), 1.0, 5.0, ((1, 64),), jnp.float32)
    dec_weight = bell_draw(splits[4], (PAIRS, F, D), (2 * BLOCK * K) ** -0.5, 0.09375, ((1, 64), (2, 8)))
    top_blocks = draw_top_blocks(jax.random.fold_in(splits[7], 71), 0)
    pair_mask = draw_pair_mask(jax.random.fold_in(splits[7], 71), 0)
    return {"activations": activations, "targets": targets, "enc_weight": enc_weight, "enc_bias": enc_bias, "dec_weight": dec_weight, "top_blocks": top_blocks, "pair_mask": pair_mask}


def pair_index(source, later):
    return source * LAYERS - source * (source - 1) // 2 + later - source

def reference(activations, targets, enc_weight, enc_bias, dec_weight, top_blocks, pair_mask):
    block_ids = jnp.arange(F // BLOCK, dtype=jnp.int32)
    block_hits = jnp.any(top_blocks[..., None] == block_ids, axis=2)
    active = jnp.repeat(block_hits.astype(jnp.float32), BLOCK, axis=-1)
    pair_gate = jnp.repeat(pair_mask.astype(jnp.float32), BLOCK, axis=-1)
    loss_scale = 1.0 / math.sqrt(ROWS)
    code_list = []
    for source in range(LAYERS):
        preact = jnp.dot(activations[:, source], enc_weight[source], preferred_element_type=jnp.float32) + enc_bias[source]
        code_list.append((active[:, source] * preact).astype(jnp.bfloat16))
    recon_list = []
    error_list = []
    for later in range(LAYERS):
        decoded = jnp.zeros((ROWS, D), jnp.float32)
        for source in range(later + 1):
            gated = code_list[source] * pair_gate[source, later].astype(jnp.bfloat16)[None]
            decoded = decoded + jnp.dot(gated, dec_weight[pair_index(source, later)], preferred_element_type=jnp.float32)
        recon_list.append(decoded.astype(jnp.bfloat16))
        error_list.append((decoded - targets[:, later].astype(jnp.float32)).astype(jnp.bfloat16))
    grad_list = []
    for source in range(LAYERS):
        code_grad = jnp.zeros((ROWS, F), jnp.float32)
        for later in range(source, LAYERS):
            code_grad = code_grad + pair_gate[source, later][None] * jnp.dot(error_list[later], dec_weight[pair_index(source, later)].T, preferred_element_type=jnp.float32)
        pre_grad = (active[:, source] * code_grad * loss_scale).astype(jnp.bfloat16)
        grad_list.append(jnp.dot(activations[:, source].T, pre_grad, preferred_element_type=jnp.float32))
    return (jnp.stack(recon_list, 1), jnp.stack(grad_list, 0))
```

```python
import functools
import math

import jax
import jax.numpy as jnp
from jax import lax
from jax.experimental import pallas as pl
from jax.experimental.pallas import tpu as pltpu
from jax.sharding import PartitionSpec as P

BLOCK = 128
LANES = 128
F32 = jnp.float32
BF16 = jnp.bfloat16
MESH = pl.DeviceIdType.MESH


def kernel(
    nz, nf, scale,
    act, tgt, enc_hbm, bias, dec_hbm, mask, gate,
    recon, a_all, pre_grad,
    enc, dec, x1, x2, xf, err_all, pf, gf,
    s1, r1, codes, s2, r2,
    core_out, core_in, right_out, right_in, left_out, left_in, y_out, y_in,
    load_sem, ag_recv1, ag_recv2, ag_right, ag_left, ag_core, y_send, y_recv,
    f_send, f_recv, core_send, core_recv, rs_rs, rs_rr, rs_ls, rs_lr,
):
    feat = lax.axis_index("feature")
    lat = lax.axis_index("latent")
    core = lat % 2
    yh = (lat // 2) % 2
    z = lat // 4
    hr, hl = nz // 2, nz // 2 - 1
    rb = act.shape[0]
    rows = a_all.shape[1]
    depth = a_all.shape[2]
    chunks = depth // LANES
    stride = 2 * chunks
    latents = enc.shape[2]
    fb = 2 * rows // nf

    def block(zz, yy, cc):
        return (zz * 2 + yy) * 2 + cc

    def zmod(v):
        return (v + nz) % nz

    right = {"latent": block(zmod(z + 1), yh, core)}
    left = {"latent": block(zmod(z - 1), yh, core)}
    other_y = {"latent": block(z, 1 - yh, core)}
    other_core = {"latent": block(z, yh, 1 - core)}

    def peer(i):
        return (feat + i) % nf

    barrier = pltpu.get_barrier_semaphore()
    for device in (right, left, other_y, other_core):
        pl.semaphore_signal(barrier, inc=1, device_id=device, device_id_type=MESH)
    for i in range(1, nf):
        pl.semaphore_signal(barrier, inc=1, device_id={"feature": peer(i)}, device_id_type=MESH)

    load_enc = pltpu.make_async_copy(enc_hbm, enc, load_sem.at[0])
    load_dec = pltpu.make_async_copy(dec_hbm, dec, load_sem.at[1])
    load_enc.start()
    load_dec.start()
    x1[lat] = act[...]
    pl.semaphore_wait(barrier, 4 + nf - 1)

    def remote(src, dst, send, recv, device):
        return pltpu.make_async_remote_copy(
            src_ref=src, dst_ref=dst, send_sem=send, recv_sem=recv, device_id=device, device_id_type=MESH
        )

    def gather(x, recv):
        def copy(b, send, device):
            return remote(x.at[b], x.at[b], send.at[b // 4 * 2 + (b // 2) % 2], recv.at[b], device)

        def y_copy():
            return remote(x.at[lat], x.at[lat], y_send, recv.at[lat], other_y)

        def arrived(b):
            copy(b, ag_right, right).wait_recv()

        copy(lat, ag_right, right).start()
        copy(lat, ag_left, left).start()
        y_copy().start()
        copy(lat, ag_core, other_core).start()
        twin = block(z, 1 - yh, core)
        arrived(twin)
        copy(twin, ag_right, right).start()
        copy(twin, ag_left, left).start()
        copy(twin, ag_core, other_core).start()

        def step(s, carry):
            for yy in (yh, 1 - yh):
                from_left = block(zmod(z - s), yy, core)
                arrived(from_left)
                copy(from_left, ag_right, right).start()
                copy(from_left, ag_core, other_core).start()
                from_right = block(zmod(z + s), yy, core)
                arrived(from_right)

                @pl.when(s < hl)
                def _():
                    copy(from_right, ag_left, left).start()

                copy(from_right, ag_core, other_core).start()
            return carry

        lax.fori_loop(1, hl + 1, step, 0)
        for yy in (yh, 1 - yh):
            last = block(zmod(z - hr), yy, core)
            arrived(last)
            copy(last, ag_core, other_core).start()

        def finish(i, carry):
            arrived(i * 2 + 1 - core)
            copy(i * 2 + core, ag_core, other_core).wait_send()
            return carry

        lax.fori_loop(0, 2 * nz, finish, 0)

        def finish_sends(s, carry):
            for yy in (yh, 1 - yh):
                copy(block(zmod(z - s), yy, core), ag_right, right).wait_send()

                @pl.when(s < hl)
                def _():
                    copy(block(zmod(z + s), yy, core), ag_left, left).wait_send()
            return carry

        lax.fori_loop(0, hr, finish_sends, 0)
        y_copy().wait_send()

    def unpack(x, out):
        def widen(b, carry):
            xf[pl.ds(pl.multiple_of(b * rb, 8), rb), :] = x[b].astype(F32)
            return carry

        lax.fori_loop(0, 4 * nz, widen, 0)
        for layer in range(2):
            for k in range(chunks):
                out[layer, :, k * LANES:(k + 1) * LANES] = xf[
                    pl.ds(layer * chunks + k, rows, stride=stride), :
                ].astype(BF16)

    def exchange(src, dst, which, own_slot):
        def copy(j):
            return remote(
                src.at[feat if own_slot else j], dst.at[feat],
                f_send.at[which, j], f_recv.at[which, feat], {"feature": j},
            )

        for i in range(1, nf):
            copy(peer(i)).start()

        def wait_from(j):
            remote(src.at[j], dst.at[j], f_send.at[which, j], f_recv.at[which, j], {"feature": j}).wait_recv()

        def wait_sent():
            for i in range(1, nf):
                copy(peer(i)).wait_send()

        return wait_from, wait_sent

    def feature_sum(part, out, inbox, which):
        for j in range(nf):
            out[j] = part[j * fb:(j + 1) * fb, :].astype(BF16)
        wait_from, wait_sent = exchange(out, inbox, which, False)
        total = part[pl.ds(pl.multiple_of(feat * fb, 8), fb), :]
        for i in range(1, nf):
            wait_from(peer(i))
            total = total + inbox[peer(i)].astype(F32)
        wait_sent()
        return total

    def share(out, which):
        wait_from, wait_sent = exchange(out, out, which, True)
        for i in range(1, nf):
            wait_from(peer(i))
        wait_sent()

    gather(x1, ag_recv1)
    unpack(x1, a_all)
    load_enc.wait()
    for layer in range(2):
        pf[layer * rows:(layer + 1) * rows, :] = jnp.dot(a_all[layer], enc[layer], preferred_element_type=F32)
    total = feature_sum(pf, s1, r1, 0)
    codes[feat] = (mask[...] * (total + bias[...])).astype(BF16)
    share(codes, 1)

    half = nf // 2
    c0 = codes[0:half].reshape(rows, latents)
    c1 = codes[half:nf].reshape(rows, latents)
    c01 = (c0.astype(F32) * gate[...]).astype(BF16)
    load_dec.wait()
    wide = 2 * LANES
    for n in range(depth // wide):
        cols = slice(n * wide, (n + 1) * wide)
        d0 = jnp.dot(c0, dec[0, :, cols], preferred_element_type=F32)
        d1 = jnp.dot(c01, dec[1, :, cols], preferred_element_type=F32)
        d1 = d1 + jnp.dot(c1, dec[2, :, cols], preferred_element_type=F32)
        for k in range(2):
            lanes = slice(k * LANES, (k + 1) * LANES)
            xf[pl.ds(2 * n + k, rows, stride=stride), :] = d0[:, lanes]
            xf[pl.ds(chunks + 2 * n + k, rows, stride=stride), :] = d1[:, lanes]

    def local(b):
        return xf[pl.ds(pl.multiple_of(b * rb, 8), rb), :]

    def core_copy(d):
        return remote(core_out.at[d], core_in.at[d], core_send.at[d], core_recv.at[d], other_core)

    def send_core(d):
        for yy in range(2):
            core_out[d, yy] = local(block(d, yy, 1 - core)).astype(BF16)
        core_copy(d).start()

    def send_cores(s, carry):
        send_core(zmod(z + hr + 1 - s))

        @pl.when(s <= hl)
        def _():
            send_core(zmod(z - hl - 1 + s))
        return carry

    lax.fori_loop(1, hr + 1, send_cores, 0)
    send_core(z)

    def right_copy(s, yy):
        return remote(right_out.at[s, yy], right_in.at[s, yy], rs_rs.at[s, yy], rs_rr.at[s, yy], right)

    def left_copy(s, yy):
        return remote(left_out.at[s, yy], left_in.at[s, yy], rs_ls.at[s, yy], rs_lr.at[s, yy], left)

    def ring(s, d, copy, out, into):
        core_copy(d).wait_recv()
        for yy in range(2):
            value = local(block(d, yy, core)) + core_in[d, yy].astype(F32)

            @pl.when(s == 0)
            def _():
                out[s, yy] = value.astype(BF16)

            @pl.when(s > 0)
            def _():
                copy(s - 1, yy).wait_recv()
                out[s, yy] = (value + into[s - 1, yy].astype(F32)).astype(BF16)

            copy(s, yy).start()

    def ring_step(s, carry):
        ring(s, zmod(z + hr - s), right_copy, right_out, right_in)

        @pl.when(s < hl)
        def _():
            ring(s, zmod(z - hl + s), left_copy, left_out, left_in)
        return carry

    lax.fori_loop(0, hr, ring_step, 0)
    core_copy(z).wait_recv()
    for yy in range(2):
        right_copy(hr - 1, yy).wait_recv()
        left_copy(hl - 1, yy).wait_recv()

    def final(yy):
        value = local(block(z, yy, core)) + core_in[z, yy].astype(F32)
        return value + right_in[hr - 1, yy].astype(F32) + left_in[hl - 1, yy].astype(F32)

    y_out[...] = final(1 - yh)
    y_copy = remote(y_out, y_in, y_send, y_recv, other_y)
    y_copy.start()
    mine = final(yh)
    y_copy.wait_recv()
    decoded = mine + y_in[...]
    recon[...] = decoded.astype(BF16)
    x2[lat] = (decoded - tgt[...].astype(F32)).astype(BF16)
    y_copy.wait_send()

    def finish_cores(d, carry):
        core_copy(d).wait_send()
        return carry

    lax.fori_loop(0, nz, finish_cores, 0)

    def finish_ring(s, carry):
        for yy in range(2):
            right_copy(s, yy).wait_send()

            @pl.when(s < hl)
            def _():
                left_copy(s, yy).wait_send()
        return carry

    lax.fori_loop(0, hr, finish_ring, 0)

    gather(x2, ag_recv2)
    unpack(x2, err_all)
    across = (((1,), (1,)), ((), ()))
    g0 = lax.dot_general(err_all[0], dec[0], across, preferred_element_type=F32)
    g01 = lax.dot_general(err_all[1], dec[1], across, preferred_element_type=F32)
    gf[0:rows, :] = g0 + gate[...] * g01
    gf[rows:2 * rows, :] = lax.dot_general(err_all[1], dec[2], across, preferred_element_type=F32)
    total = feature_sum(gf, s2, r2, 2)
    pre_grad[feat] = (mask[...] * total * scale).astype(BF16)
    share(pre_grad, 3)


def body(nz, nf, activations, targets, enc_weight, enc_bias, dec_weight, top_blocks, pair_mask):
    own_rows, layers, depth = activations.shape
    rows = top_blocks.shape[0]
    latents = enc_weight.shape[2]
    local_blocks = latents // BLOCK
    chunks = depth // LANES
    rb = own_rows * layers * chunks
    fb = layers * rows // nf
    first_block = lax.axis_index("latent") * local_blocks
    feat = lax.axis_index("feature")
    block_ids = first_block + jnp.arange(local_blocks, dtype=jnp.int32)
    top = lax.dynamic_slice_in_dim(top_blocks.transpose(1, 0, 2).reshape(layers * rows, -1), feat * fb, fb, 0)
    hits = jnp.any(top[..., None] == block_ids, axis=1)
    mask = jnp.repeat(hits.astype(F32), BLOCK, axis=-1)
    gate = lax.dynamic_slice_in_dim(pair_mask[0, 1], first_block, local_blocks, 0)
    gate = jnp.repeat(gate.astype(F32), BLOCK)[None]
    bias = lax.dynamic_slice_in_dim(enc_bias, feat * layers // nf, 1, 0)
    hr, hl = nz // 2, nz // 2 - 1
    blocks = 4 * nz
    vmem = pl.BlockSpec(memory_space=pltpu.VMEM)
    hbm = pl.BlockSpec(memory_space=pl.ANY)
    dma = pltpu.SemaphoreType.DMA
    recon, a_all, pre_grad = pl.pallas_call(
        functools.partial(kernel, nz, nf, 1.0 / math.sqrt(rows)),
        out_shape=(
            jax.ShapeDtypeStruct((rb, LANES), BF16),
            jax.ShapeDtypeStruct((layers, rows, depth), BF16),
            jax.ShapeDtypeStruct((nf, fb, latents), BF16),
        ),
        in_specs=[vmem, vmem, hbm, vmem, hbm, vmem, vmem],
        out_specs=(vmem, vmem, vmem),
        scratch_shapes=[
            pltpu.VMEM(enc_weight.shape, BF16),
            pltpu.VMEM(dec_weight.shape, BF16),
            pltpu.VMEM((blocks, rb, LANES), BF16),
            pltpu.VMEM((blocks, rb, LANES), BF16),
            pltpu.VMEM((blocks * rb, LANES), F32),
            pltpu.VMEM((layers, rows, depth), BF16),
            pltpu.VMEM((layers * rows, latents), F32),
            pltpu.VMEM((layers * rows, latents), F32),
            pltpu.VMEM((nf, fb, latents), BF16),
            pltpu.VMEM((nf, fb, latents), BF16),
            pltpu.VMEM((nf, fb, latents), BF16),
            pltpu.VMEM((nf, fb, latents), BF16),
            pltpu.VMEM((nf, fb, latents), BF16),
            pltpu.VMEM((nz, 2, rb, LANES), BF16),
            pltpu.VMEM((nz, 2, rb, LANES), BF16),
            pltpu.VMEM((hr, 2, rb, LANES), BF16),
            pltpu.VMEM((hr, 2, rb, LANES), BF16),
            pltpu.VMEM((hl, 2, rb, LANES), BF16),
            pltpu.VMEM((hl, 2, rb, LANES), BF16),
            pltpu.VMEM((rb, LANES), F32),
            pltpu.VMEM((rb, LANES), F32),
            dma((2,)),
            dma((blocks,)),
            dma((blocks,)),
            dma((2 * nz,)),
            dma((2 * nz,)),
            dma((2 * nz,)),
            dma,
            dma,
            dma((4, nf)),
            dma((4, nf)),
            dma((nz,)),
            dma((nz,)),
            dma((hr, 2)),
            dma((hr, 2)),
            dma((hl, 2)),
            dma((hl, 2)),
        ],
        compiler_params=pltpu.CompilerParams(
            collective_id=0, has_side_effects=True, vmem_limit_bytes=48 * 2**20
        ),
    )(
        activations.reshape(rb, LANES), targets.reshape(rb, LANES), enc_weight, bias, dec_weight, mask, gate
    )
    enc_grad = jnp.einsum(
        "lrd,lrf->ldf", a_all, pre_grad.reshape(layers, rows, latents), preferred_element_type=F32
    )
    return recon.reshape(own_rows, layers, depth), enc_grad


def solution(mesh):
    in_specs = (
        P("latent", None, "feature"),
        P("latent", None, "feature"),
        P(None, "feature", "latent"),
        P(None, "latent"),
        P(None, "latent", "feature"),
        P(),
        P(),
    )
    out_specs = (P("latent", None, "feature"), P(None, "feature", "latent"))
    step = functools.partial(body, mesh.shape["latent"] // 4, mesh.shape["feature"])
    return jax.shard_map(step, mesh=mesh, in_specs=in_specs, out_specs=out_specs, check_vma=False)
```

```python
import functools
import math

import jax
import jax.numpy as jnp
from jax import lax
from jax.experimental import pallas as pl
from jax.experimental.pallas import tpu as pltpu
from jax.sharding import PartitionSpec as P

BLOCK = 128
LANES = 128
F32 = jnp.float32
BF16 = jnp.bfloat16
MESH = pl.DeviceIdType.MESH
NEAR = 4
MESSAGES = (
    (1, 0, "all", 0), (1, 1, "all", 1), (-1, 0, "all", 2), (-1, 1, "all", 3),
    (2, 0, "low", 4), (2, 1, "low", 5), (-2, 0, "high", 4), (-2, 1, "high", 5),
    (0, 1, "all", 6),
)
SLOTS = 7


def kernel(
    nz, nf, scale,
    act, tgt, enc_hbm, bias, dec_hbm, mask, gate,
    recon, a_all, pre_out,
    enc, dec, x, xf, err_all, part, grad,
    f_out, f_in, codes, pre_grad,
    core_out, core_in, near_out, near_in, total, far_out, far_in,
    load_sem, far_s, far_r, near_s, near_r, core_s, core_r,
    f_send, f_recv, rc_s, rc_r, rn_s, rn_r, rf_s, rf_r,
):
    feat = lax.axis_index("feature")
    lat = lax.axis_index("latent")
    c = lat % 2
    y = (lat // 2) % 2
    z = lat // 4
    nq = nz // NEAR
    q, m = z // NEAR, z % NEAR
    rb = act.shape[1]
    rows, depth = a_all.shape[1:]
    chunks = depth // LANES
    latents = enc.shape[2]
    fb = rows // nf
    group = nq * rb

    def at(zz, yy, cc):
        return {"latent": (((zz + nz) % nz) * 2 + yy) * 2 + cc}

    other_core = at(z, y, 1 - c)
    near_devices = [at(z + dz, 1 - y if dy else y, c) for dz, dy, _, _ in MESSAGES]
    far_devices = [at(z + NEAR * j, y, c) for j in range(1, nq)]
    parts = {"all": slice(0, nq), "low": slice(0, nq // 2), "high": slice(nq // 2, nq)}

    def span(which):
        s = parts[which]
        return pl.ds(s.start, s.stop - s.start)

    def peer(i):
        return (feat + i) % nf

    feature_devices = [{"feature": peer(i)} for i in range(1, nf)]
    everyone = [other_core] + near_devices + far_devices + feature_devices
    barrier = pltpu.get_barrier_semaphore()
    for device in everyone:
        pl.semaphore_signal(barrier, inc=1, device_id=device, device_id_type=MESH)
    load_enc = pltpu.make_async_copy(enc_hbm, enc, load_sem.at[0])
    load_dec = pltpu.make_async_copy(dec_hbm, dec, load_sem.at[1])
    load_enc.start()
    load_dec.start()
    for t in range(2):
        x[0, t, m, y, c, q] = act[t]
    pl.semaphore_wait(barrier, len(everyone))

    def remote(src, dst, send, recv, device):
        return pltpu.make_async_remote_copy(
            src_ref=src, dst_ref=dst, send_sem=send, recv_sem=recv, device_id=device, device_id_type=MESH
        )

    def far_copy(g, t, j):
        ref = x.at[g, t, m, y, c, q]
        return remote(ref, ref, far_s.at[g, t, j], far_r.at[g, t, j], far_devices[j - 1])

    def far_arrival(g, t, j):
        ref = x.at[g, t, m, y, c, (q - j + nq) % nq]
        return remote(ref, ref, far_s.at[g, t, j], far_r.at[g, t, j], far_devices[j - 1])

    def near_copy(g, t, n):
        ref = x.at[g, t, m, y, c, span(MESSAGES[n][2])]
        return remote(ref, ref, near_s.at[g, t, n], near_r.at[g, t, n], near_devices[n])

    def arrival_ref(g, t, n, cc):
        if n == len(MESSAGES):
            return x.at[g, t, m, y, cc]
        dz, dy, which, _ = MESSAGES[n]
        return x.at[g, t, (m - dz + NEAR) % NEAR, 1 - y if dy else y, cc, span(which)]

    def near_arrival(g, t, n):
        ref = arrival_ref(g, t, n, c)
        return remote(ref, ref, near_s.at[g, t, n], near_r.at[g, t, n], near_devices[n])

    def core_copy(g, t, n, cc):
        ref = arrival_ref(g, t, n, cc)
        return remote(ref, ref, core_s.at[g, t, n], core_r.at[g, t, n], other_core)

    def gather_far(g, t):
        for j in range(1, nq):
            far_copy(g, t, j).start()

    def gather_near(g, t):
        for j in range(1, nq):
            far_arrival(g, t, j).wait_recv()
        for n in range(len(MESSAGES)):
            near_copy(g, t, n).start()
        core_copy(g, t, len(MESSAGES), c).start()

    def gather_core(g, t):
        for n in range(len(MESSAGES)):
            near_arrival(g, t, n).wait_recv()
            core_copy(g, t, n, c).start()

    def gather_end(g, t, out):
        for n in range(len(MESSAGES) + 1):
            core_copy(g, t, n, 1 - c).wait_recv()

        def widen(i, carry):
            blocks = x[g, t, i // 4, (i // 2) % 2, i % 2].astype(F32)
            xf[t, pl.ds(pl.multiple_of(i * group, 8), group), :] = blocks.reshape(group, LANES)
            return carry

        lax.fori_loop(0, 4 * NEAR, widen, 0)
        for k in range(chunks):
            out[t, :, k * LANES:(k + 1) * LANES] = xf[t, pl.ds(k, rows, stride=chunks), :].astype(BF16)

    def gather_sent(g, t):
        for j in range(1, nq):
            far_copy(g, t, j).wait_send()
        for n in range(len(MESSAGES)):
            near_copy(g, t, n).wait_send()
        for n in range(len(MESSAGES) + 1):
            core_copy(g, t, n, c).wait_send()

    def sum_copy(g, t, i):
        j = peer(i)
        return remote(
            f_out.at[g, t, j], f_in.at[g, t, i], f_send.at[0, g, t, i], f_recv.at[0, g, t, i], feature_devices[i - 1]
        )

    def sum_start(g, t, values):
        for j in range(nf):
            f_out[g, t, j] = values[t, j * fb:(j + 1) * fb, :].astype(BF16)
        for i in range(1, nf):
            sum_copy(g, t, i).start()

    def sum_end(g, t, values):
        acc = values[t, pl.ds(pl.multiple_of(feat * fb, 8), fb), :]
        for i in range(1, nf):
            sum_copy(g, t, i).wait_recv()
            acc = acc + f_in[g, t, i].astype(F32)
        return acc

    def share_copy(g, t, ref, i, mine):
        slot = ref.at[t, feat if mine else (feat - i + nf) % nf]
        return remote(slot, slot, f_send.at[1, g, t, i], f_recv.at[1, g, t, i], feature_devices[i - 1])

    def share_start(g, t, ref):
        for i in range(1, nf):
            share_copy(g, t, ref, i, True).start()

    def share_end(g, t, ref):
        for i in range(1, nf):
            share_copy(g, t, ref, i, False).wait_recv()

    def feature_sent(g, t, ref):
        for i in range(1, nf):
            sum_copy(g, t, i).wait_send()
            share_copy(g, t, ref, i, True).wait_send()

    def local(t, mm, yy, cc):
        start = ((mm * 2 + yy) * 2 + cc) * group
        return xf[t, pl.ds(pl.multiple_of(start, 8), group), :]

    def blocks(value):
        return value.reshape(nq, rb, LANES)

    steps = (1, -1, 2, 0)

    def rc_copy(t, s):
        mm = (m + steps[s] + NEAR) % NEAR
        return remote(core_out.at[t, mm], core_in.at[t, mm], rc_s.at[t, s], rc_r.at[t, s], other_core)

    def reduce_core(t):
        for s in range(NEAR):
            mm = (m + steps[s] + NEAR) % NEAR
            for yy in range(2):
                core_out[t, mm, yy] = blocks(local(t, mm, yy, 1 - c)).astype(BF16)
            rc_copy(t, s).start()

    def with_core(t, mm, yy):
        return blocks(local(t, mm, yy, c)) + core_in[t, mm, yy].astype(F32)

    def rn_copy(t, n):
        dz, dy, which, slot = MESSAGES[n]
        mm = (m + dz + NEAR) % NEAR
        yy = 1 - y if dy else y
        return remote(
            near_out.at[t, mm, yy, span(which)], near_in.at[t, slot, span(which)],
            rn_s.at[t, n], rn_r.at[t, n], near_devices[n],
        )

    def reduce_near(t):
        for s, messages in enumerate(((0, 1), (2, 3), (4, 5, 6, 7), (8,))):
            mm = (m + steps[s] + NEAR) % NEAR
            rc_copy(t, s).wait_recv()
            for yy in ((y, 1 - y) if s < 3 else (1 - y,)):
                near_out[t, mm, yy] = with_core(t, mm, yy).astype(BF16)
            for n in messages:
                rn_copy(t, n).start()

    def rf_copy(t, j):
        return remote(far_out.at[t, j], far_in.at[t, j], rf_s.at[t, j], rf_r.at[t, j], far_devices[j - 1])

    def reduce_far(t):
        for n in range(len(MESSAGES)):
            rn_copy(t, n).wait_recv()
        acc = with_core(t, m, y)
        for slot in range(SLOTS):
            acc = acc + near_in[t, slot].astype(F32)
        total[t] = acc
        for j in range(1, nq):
            far_out[t, j] = total[t, (q + j) % nq].astype(BF16)
            rf_copy(t, j).start()

    def reduce_end(t):
        acc = total[t, q]
        for j in range(1, nq):
            rf_copy(t, j).wait_recv()
            acc = acc + far_in[t, j].astype(F32)
        recon[t] = acc.astype(BF16)
        x[1, t, m, y, c, q] = (acc - tgt[t].astype(F32)).astype(BF16)

    def reduce_sent(t):
        for s in range(NEAR):
            rc_copy(t, s).wait_send()
        for n in range(len(MESSAGES)):
            rn_copy(t, n).wait_send()
        for j in range(1, nq):
            rf_copy(t, j).wait_send()

    both = (0, 1)
    for t in both:
        gather_far(0, t)
    for t in both:
        gather_near(0, t)
    load_enc.wait()
    for t in both:
        gather_core(0, t)
    for t in both:
        gather_end(0, t, a_all)
        part[t] = jnp.dot(a_all[t], enc[t], preferred_element_type=F32)
        sum_start(0, t, part)
    for t in both:
        codes[t, feat] = (mask[t] * (sum_end(0, t, part) + bias[t:t + 1, :])).astype(BF16)
        share_start(0, t, codes)
    load_dec.wait()

    def whole(t):
        return codes[t].astype(F32).reshape(rows, latents)

    wide = 2 * LANES
    for t in both:
        share_end(0, t, codes)
        if t == 0:
            terms = ((whole(0).astype(BF16), 0),)
        else:
            terms = (((whole(0) * gate[...]).astype(BF16), 1), (whole(1).astype(BF16), 2))
        for n in range(depth // wide):
            cols = slice(n * wide, (n + 1) * wide)
            value = sum(jnp.dot(code, dec[p, :, cols], preferred_element_type=F32) for code, p in terms)
            for k in range(2):
                xf[t, pl.ds(2 * n + k, rows, stride=chunks), :] = value[:, k * LANES:(k + 1) * LANES]
        reduce_core(t)
    for t in both:
        reduce_near(t)
    for t in both:
        gather_sent(0, t)
        feature_sent(0, t, codes)
    for t in both:
        reduce_far(t)
    for t in both:
        reduce_end(t)
        gather_far(1, t)
    for t in both:
        gather_near(1, t)
    for t in both:
        reduce_sent(t)
    for t in both:
        gather_core(1, t)
    across = (((1,), (1,)), ((), ()))
    gather_end(1, 0, err_all)
    grad[0] = lax.dot_general(err_all[0], dec[0], across, preferred_element_type=F32)
    gather_end(1, 1, err_all)
    grad[1] = lax.dot_general(err_all[1], dec[2], across, preferred_element_type=F32)
    sum_start(1, 1, grad)
    grad[0] = grad[0] + gate[...] * lax.dot_general(err_all[1], dec[1], across, preferred_element_type=F32)
    sum_start(1, 0, grad)
    for t in (1, 0):
        pre_grad[t, feat] = (mask[t] * sum_end(1, t, grad) * scale).astype(BF16)
        share_start(1, t, pre_grad)
    for t in both:
        gather_sent(1, t)
    for t in (1, 0):
        share_end(1, t, pre_grad)
        pre_out[t] = pre_grad[t].astype(F32).reshape(rows, latents).astype(BF16)
    for t in both:
        feature_sent(1, t, pre_grad)


def body(nz, nf, activations, targets, enc_weight, enc_bias, dec_weight, top_blocks, pair_mask):
    own_rows, layers, depth = activations.shape
    rows = top_blocks.shape[0]
    latents = enc_weight.shape[2]
    local_blocks = latents // BLOCK
    chunks = depth // LANES
    rb = own_rows * chunks
    fb = rows // nf
    nq = nz // NEAR
    first_block = lax.axis_index("latent") * local_blocks
    feat = lax.axis_index("feature")
    block_ids = first_block + jnp.arange(local_blocks, dtype=jnp.int32)
    top = top_blocks.reshape(nq, NEAR, 2, 2, own_rows, layers, -1).transpose(5, 1, 2, 3, 0, 4, 6)
    top = lax.dynamic_slice_in_dim(top.reshape(layers, rows, -1), feat * fb, fb, 1)
    hits = jnp.any(top[..., None] == block_ids, axis=2)
    mask = jnp.repeat(hits.astype(F32), BLOCK, axis=-1)
    gate = lax.dynamic_slice_in_dim(pair_mask[0, 1], first_block, local_blocks, 0)
    gate = jnp.repeat(gate.astype(F32), BLOCK)[None]
    vmem = pl.BlockSpec(memory_space=pltpu.VMEM)
    hbm = pl.BlockSpec(memory_space=pl.ANY)
    dma = pltpu.SemaphoreType.DMA
    bf, f32 = (lambda *s: pltpu.VMEM(s, BF16)), (lambda *s: pltpu.VMEM(s, F32))
    count = len(MESSAGES)
    recon, a_all, pre_grad = pl.pallas_call(
        functools.partial(kernel, nz, nf, 1.0 / math.sqrt(rows)),
        out_shape=(
            jax.ShapeDtypeStruct((layers, rb, LANES), BF16),
            jax.ShapeDtypeStruct((layers, rows, depth), BF16),
            jax.ShapeDtypeStruct((layers, rows, latents), BF16),
        ),
        in_specs=[vmem, vmem, hbm, vmem, hbm, vmem, vmem],
        out_specs=(vmem, vmem, vmem),
        scratch_shapes=[
            bf(*enc_weight.shape),
            bf(*dec_weight.shape),
            bf(2, layers, NEAR, 2, 2, nq, rb, LANES),
            f32(layers, rows * chunks, LANES),
            bf(layers, rows, depth),
            f32(layers, rows, latents),
            f32(layers, rows, latents),
            bf(2, layers, nf, fb, latents),
            bf(2, layers, nf, fb, latents),
            bf(layers, nf, fb, latents),
            bf(layers, nf, fb, latents),
            bf(layers, NEAR, 2, nq, rb, LANES),
            bf(layers, NEAR, 2, nq, rb, LANES),
            bf(layers, NEAR, 2, nq, rb, LANES),
            bf(layers, SLOTS, nq, rb, LANES),
            f32(layers, nq, rb, LANES),
            bf(layers, nq, rb, LANES),
            bf(layers, nq, rb, LANES),
            dma((2,)),
            dma((2, layers, nq)),
            dma((2, layers, nq)),
            dma((2, layers, count)),
            dma((2, layers, count)),
            dma((2, layers, count + 1)),
            dma((2, layers, count + 1)),
            dma((2, 2, layers, nf)),
            dma((2, 2, layers, nf)),
            dma((layers, NEAR)),
            dma((layers, NEAR)),
            dma((layers, count)),
            dma((layers, count)),
            dma((layers, nq)),
            dma((layers, nq)),
        ],
        compiler_params=pltpu.CompilerParams(
            collective_id=0, has_side_effects=True, vmem_limit_bytes=48 * 2**20
        ),
    )(
        activations.transpose(1, 0, 2).reshape(layers, rb, LANES),
        targets.transpose(1, 0, 2).reshape(layers, rb, LANES),
        enc_weight, enc_bias, dec_weight, mask, gate,
    )
    enc_grad = jnp.einsum("lrd,lrf->ldf", a_all, pre_grad, preferred_element_type=F32)
    return recon.reshape(layers, own_rows, depth).transpose(1, 0, 2), enc_grad


def solution(mesh):
    in_specs = (
        P("latent", None, "feature"),
        P("latent", None, "feature"),
        P(None, "feature", "latent"),
        P(None, "latent"),
        P(None, "latent", "feature"),
        P(),
        P(),
    )
    out_specs = (P("latent", None, "feature"), P(None, "feature", "latent"))
    step = functools.partial(body, mesh.shape["latent"] // 4, mesh.shape["feature"])
    return jax.shard_map(step, mesh=mesh, in_specs=in_specs, out_specs=out_specs, check_vma=False)
```

```python
import functools
import math

import jax
import jax.numpy as jnp
from jax import lax
from jax.experimental import pallas as pl
from jax.experimental.pallas import tpu as pltpu
from jax.sharding import PartitionSpec as P

BLOCK = 128
LANES = 128
F32 = jnp.float32
BF16 = jnp.bfloat16
MESH = pl.DeviceIdType.MESH
NEAR = 4
MESSAGES = (
    (1, 0, "all", 0), (1, 1, "all", 1), (-1, 0, "all", 2), (-1, 1, "all", 3),
    (2, 0, "low", 4), (2, 1, "low", 5), (-2, 0, "high", 4), (-2, 1, "high", 5),
    (0, 1, "all", 6),
)
SLOTS = 7


def kernel(
    nz, nf, scale,
    act, tgt, enc_hbm, bias, dec_hbm, top, pairs,
    recon, a_hbm, pre_out,
    a_all, enc, dec, own, goal, wide_rows, mask, gate, x, xf, err_all, part, grad,
    f_out, f_in, codes, pre_grad,
    core_out, core_in, near_out, near_in, total, total_rows, far_out, far_in,
    load_sem, far_s, far_r, near_s, near_r, core_s, core_r,
    f_send, f_recv, rc_s, rc_r, rn_s, rn_r, rf_s, rf_r,
):
    feat = lax.axis_index("feature")
    lat = lax.axis_index("latent")
    c = lat % 2
    y = (lat // 2) % 2
    z = lat // 4
    nq = nz // NEAR
    held = (z + 2) % NEAR
    offsets = [2 - nz // 2 + NEAR * j for j in range(nq)]
    own_rows = act.shape[0]
    rb = own.shape[2]
    rows, depth = a_all.shape[1:]
    chunks = depth // LANES
    latents = enc.shape[2]
    fb = rows // nf
    group = nq * rb

    def at(zz, yy, cc):
        return {"latent": (((zz + nz) % nz) * 2 + yy) * 2 + cc}

    other_core = at(z, y, 1 - c)
    near_devices = [at(z + dz, 1 - y if dy else y, c) for dz, dy, _, _ in MESSAGES]
    far_devices = [at(z + o, y, c) for o in offsets]
    far_blocks = [((z - o + nz) % nz) // NEAR for o in offsets]
    parts = {"all": slice(0, nq), "low": slice(0, nq // 2), "high": slice(nq // 2, nq)}

    def span(which):
        s = parts[which]
        return pl.ds(s.start, s.stop - s.start)

    def peer(i):
        return (feat + i) % nf

    feature_devices = [{"feature": peer(i)} for i in range(1, nf)]
    everyone = [other_core] + near_devices + far_devices + feature_devices
    barrier = pltpu.get_barrier_semaphore()
    for device in everyone:
        pl.semaphore_signal(barrier, inc=1, device_id=device, device_id_type=MESH)
    load_enc = pltpu.make_async_copy(enc_hbm, enc, load_sem.at[0])
    load_dec = pltpu.make_async_copy(dec_hbm, dec, load_sem.at[1])
    load_enc.start()
    load_dec.start()

    def split(ref, t, put):
        values = ref[...].astype(F32)
        for k in range(chunks):
            put[t, pl.ds(k, own_rows, stride=chunks), :] = values[:, t, k * LANES:(k + 1) * LANES]

    for t in range(2):
        split(act, t, total_rows)
        own[0, t] = total_rows[t].astype(BF16)
        split(tgt, t, goal)
    local_blocks = latents // BLOCK
    place = feat * fb + lax.broadcasted_iota(jnp.int32, (fb, rows), 0)
    index = lax.div(place, own_rows)
    device = lax.rem(index, nq) * (4 * NEAR) + lax.div(index, nq)
    picked = device * own_rows + lax.rem(place, own_rows) == lax.broadcasted_iota(jnp.int32, (fb, rows), 1)
    picked = jnp.where(picked, 1.0, 0.0).astype(BF16)
    across = (((1,), (1,)), ((), ()))
    for t in range(2):
        hits = []
        for b in range(local_blocks):
            same = jnp.where(top[t] == lat * local_blocks + b, 1.0, 0.0)
            hits.append(jnp.broadcast_to(jnp.sum(same, axis=0, keepdims=True), (BLOCK, rows)))
        hits = jnp.concatenate(hits, axis=0).astype(BF16)
        mask[t] = lax.dot_general(picked, hits, across, preferred_element_type=F32)
    numbers = pairs[0].astype(F32)[1:2]
    lanes = lax.broadcasted_iota(jnp.int32, numbers.shape, 1)
    for b in range(local_blocks):
        value = jnp.sum(jnp.where(lanes == lat * local_blocks + b, numbers, 0.0), axis=1, keepdims=True)
        gate[:, b * BLOCK:(b + 1) * BLOCK] = jnp.broadcast_to(value, (1, BLOCK))
    pl.semaphore_wait(barrier, len(everyone))

    def remote(src, dst, send, recv, device):
        return pltpu.make_async_remote_copy(
            src_ref=src, dst_ref=dst, send_sem=send, recv_sem=recv, device_id=device, device_id_type=MESH
        )

    def far_copy(g, t, j):
        ref = x.at[g, t, z % NEAR, y, c, z // NEAR]
        return remote(own.at[g, t], ref, far_s.at[g, t, j], far_r.at[g, t, j], far_devices[j])

    def far_arrival(g, t, j):
        ref = x.at[g, t, held, y, c, far_blocks[j]]
        return remote(ref, ref, far_s.at[g, t, j], far_r.at[g, t, j], far_devices[j])

    def near_copy(g, t, n):
        ref = x.at[g, t, held, y, c, span(MESSAGES[n][2])]
        return remote(ref, ref, near_s.at[g, t, n], near_r.at[g, t, n], near_devices[n])

    def arrival_ref(g, t, n, cc):
        if n == len(MESSAGES):
            return x.at[g, t, held, y, cc]
        dz, dy, which, _ = MESSAGES[n]
        return x.at[g, t, (held - dz + NEAR) % NEAR, 1 - y if dy else y, cc, span(which)]

    def near_arrival(g, t, n):
        ref = arrival_ref(g, t, n, c)
        return remote(ref, ref, near_s.at[g, t, n], near_r.at[g, t, n], near_devices[n])

    def core_copy(g, t, n, cc):
        ref = arrival_ref(g, t, n, cc)
        return remote(ref, ref, core_s.at[g, t, n], core_r.at[g, t, n], other_core)

    def gather_far(g, t):
        for j in range(nq):
            far_copy(g, t, j).start()

    def gather_near(g, t):
        for j in range(nq):
            far_arrival(g, t, j).wait_recv()
        for n in range(len(MESSAGES)):
            near_copy(g, t, n).start()
        core_copy(g, t, len(MESSAGES), c).start()

    def gather_core(g, t):
        for n in range(len(MESSAGES)):
            near_arrival(g, t, n).wait_recv()
            core_copy(g, t, n, c).start()

    def gather_end(g, t, out):
        for n in range(len(MESSAGES) + 1):
            core_copy(g, t, n, 1 - c).wait_recv()

        def widen(i, carry):
            blocks = x[g, t, i // 4, (i // 2) % 2, i % 2].astype(F32)
            xf[t, pl.ds(pl.multiple_of(i * group, 8), group), :] = blocks.reshape(group, LANES)
            return carry

        lax.fori_loop(0, 4 * NEAR, widen, 0)
        for k in range(chunks):
            out[t, :, k * LANES:(k + 1) * LANES] = xf[t, pl.ds(k, rows, stride=chunks), :].astype(BF16)

    def gather_sent(g, t):
        for j in range(nq):
            far_copy(g, t, j).wait_send()
        for n in range(len(MESSAGES)):
            near_copy(g, t, n).wait_send()
        for n in range(len(MESSAGES) + 1):
            core_copy(g, t, n, c).wait_send()

    def sum_copy(g, t, i):
        j = peer(i)
        return remote(
            f_out.at[g, t, j], f_in.at[g, t, i], f_send.at[0, g, t, i], f_recv.at[0, g, t, i], feature_devices[i - 1]
        )

    def sum_start(g, t, values):
        for j in range(nf):
            f_out[g, t, j] = values[t, j * fb:(j + 1) * fb, :].astype(BF16)
        for i in range(1, nf):
            sum_copy(g, t, i).start()

    def sum_end(g, t, values):
        acc = values[t, pl.ds(pl.multiple_of(feat * fb, 8), fb), :]
        for i in range(1, nf):
            sum_copy(g, t, i).wait_recv()
            acc = acc + f_in[g, t, i].astype(F32)
        return acc

    def share_copy(g, t, ref, i, mine):
        slot = ref.at[t, feat if mine else (feat - i + nf) % nf]
        return remote(slot, slot, f_send.at[1, g, t, i], f_recv.at[1, g, t, i], feature_devices[i - 1])

    def share_start(g, t, ref):
        for i in range(1, nf):
            share_copy(g, t, ref, i, True).start()

    def share_end(g, t, ref):
        for i in range(1, nf):
            share_copy(g, t, ref, i, False).wait_recv()

    def feature_sent(g, t, ref):
        for i in range(1, nf):
            sum_copy(g, t, i).wait_send()
            share_copy(g, t, ref, i, True).wait_send()

    def local(t, mm, yy, cc):
        start = ((mm * 2 + yy) * 2 + cc) * group
        return xf[t, pl.ds(pl.multiple_of(start, 8), group), :]

    def blocks(value):
        return value.reshape(nq, rb, LANES)

    steps = (1, -1, 2, 0)

    def rc_copy(t, s):
        mm = (held + steps[s] + NEAR) % NEAR
        return remote(core_out.at[t, mm], core_in.at[t, mm], rc_s.at[t, s], rc_r.at[t, s], other_core)

    def reduce_core(t):
        for s in range(NEAR):
            mm = (held + steps[s] + NEAR) % NEAR
            for yy in range(2):
                core_out[t, mm, yy] = blocks(local(t, mm, yy, 1 - c)).astype(BF16)
            rc_copy(t, s).start()

    def with_core(t, mm, yy):
        return blocks(local(t, mm, yy, c)) + core_in[t, mm, yy].astype(F32)

    def rn_copy(t, n):
        dz, dy, which, slot = MESSAGES[n]
        mm = (held + dz + NEAR) % NEAR
        yy = 1 - y if dy else y
        return remote(
            near_out.at[t, mm, yy, span(which)], near_in.at[t, slot, span(which)],
            rn_s.at[t, n], rn_r.at[t, n], near_devices[n],
        )

    def reduce_near(t):
        for s, messages in enumerate(((0, 1), (2, 3), (4, 5, 6, 7), (8,))):
            mm = (held + steps[s] + NEAR) % NEAR
            rc_copy(t, s).wait_recv()
            for yy in ((y, 1 - y) if s < 3 else (1 - y,)):
                near_out[t, mm, yy] = with_core(t, mm, yy).astype(BF16)
            for n in messages:
                rn_copy(t, n).start()

    def rf_copy(t, j):
        return remote(far_out.at[t, j], far_in.at[t, j], rf_s.at[t, j], rf_r.at[t, j], far_devices[nq - 1 - j])

    def reduce_far(t):
        for n in range(len(MESSAGES)):
            rn_copy(t, n).wait_recv()
        acc = with_core(t, held, y)
        for slot in range(SLOTS):
            acc = acc + near_in[t, slot].astype(F32)
        total[t] = acc
        for j in range(nq):
            far_out[t, j] = total[t, far_blocks[j]].astype(BF16)
            rf_copy(t, j).start()

    def reduce_end(t):
        acc = jnp.zeros((rb, LANES), F32)
        for j in range(nq):
            rf_copy(t, j).wait_recv()
            acc = acc + far_in[t, j].astype(F32)
        own[1, t] = (acc - goal[t]).astype(BF16)
        total_rows[t] = acc

    def write_recon(t):
        for k in range(chunks):
            wide_rows[:, t, k * LANES:(k + 1) * LANES] = total_rows[t, pl.ds(k, own_rows, stride=chunks), :]

    def reduce_sent(t):
        for s in range(NEAR):
            rc_copy(t, s).wait_send()
        for n in range(len(MESSAGES)):
            rn_copy(t, n).wait_send()
        for j in range(nq):
            rf_copy(t, j).wait_send()

    both = (0, 1)
    for t in both:
        gather_far(0, t)
    for t in both:
        gather_near(0, t)
    load_enc.wait()
    for t in both:
        gather_core(0, t)
        gather_end(0, t, a_all)
        part[t] = jnp.dot(a_all[t], enc[t], preferred_element_type=F32)
        sum_start(0, t, part)
    store_act = [pltpu.make_async_copy(a_all.at[t], a_hbm.at[t], load_sem.at[2 + t]) for t in both]
    for t in both:
        store_act[t].start()
        codes[t, feat] = (mask[t] * (sum_end(0, t, part) + bias[t:t + 1, :])).astype(BF16)
        share_start(0, t, codes)
    load_dec.wait()

    def whole(t):
        return codes[t].astype(F32).reshape(rows, latents)

    wide = 2 * LANES
    for t in both:
        share_end(0, t, codes)
        if t == 0:
            terms = ((whole(0).astype(BF16), 0),)
        else:
            terms = (((whole(0) * gate[...]).astype(BF16), 1), (whole(1).astype(BF16), 2))
        for n in range(depth // wide):
            cols = slice(n * wide, (n + 1) * wide)
            value = sum(jnp.dot(code, dec[p, :, cols], preferred_element_type=F32) for code, p in terms)
            for k in range(2):
                xf[t, pl.ds(2 * n + k, rows, stride=chunks), :] = value[:, k * LANES:(k + 1) * LANES]
        reduce_core(t)
    for t in both:
        reduce_near(t)
    for t in both:
        gather_sent(0, t)
        feature_sent(0, t, codes)
    for t in both:
        reduce_far(t)
    for t in both:
        reduce_end(t)
        gather_far(1, t)
    for t in both:
        gather_near(1, t)
    for t in both:
        reduce_sent(t)
        write_recon(t)
    recon[...] = wide_rows[...].astype(BF16)
    gather_core(1, 0)
    gather_end(1, 0, err_all)
    grad[0] = lax.dot_general(err_all[0], dec[0], across, preferred_element_type=F32)
    gather_core(1, 1)
    gather_end(1, 1, err_all)
    grad[1] = lax.dot_general(err_all[1], dec[2], across, preferred_element_type=F32)
    sum_start(1, 1, grad)
    grad[0] = grad[0] + gate[...] * lax.dot_general(err_all[1], dec[1], across, preferred_element_type=F32)
    sum_start(1, 0, grad)
    for t in (1, 0):
        pre_grad[t, feat] = (mask[t] * sum_end(1, t, grad) * scale).astype(BF16)
        share_start(1, t, pre_grad)
    for t in both:
        gather_sent(1, t)
    for t in (1, 0):
        share_end(1, t, pre_grad)
        pre_out[t] = pre_grad[t].astype(F32).reshape(rows, latents).astype(BF16)
    for t in both:
        feature_sent(1, t, pre_grad)
        store_act[t].wait()


def body(nz, nf, activations, targets, enc_weight, enc_bias, dec_weight, top_blocks, pair_mask):
    own_rows, layers, depth = activations.shape
    rows = top_blocks.shape[0]
    latents = enc_weight.shape[2]
    local_blocks = latents // BLOCK
    chunks = depth // LANES
    rb = own_rows * chunks
    fb = rows // nf
    nq = nz // NEAR
    vmem = pl.BlockSpec(memory_space=pltpu.VMEM)
    hbm = pl.BlockSpec(memory_space=pltpu.HBM)
    dma = pltpu.SemaphoreType.DMA
    bf, f32 = (lambda *s: pltpu.VMEM(s, BF16)), (lambda *s: pltpu.VMEM(s, F32))
    count = len(MESSAGES)
    recon, a_all, pre_grad = pl.pallas_call(
        functools.partial(kernel, nz, nf, 1.0 / math.sqrt(rows)),
        out_shape=(
            jax.ShapeDtypeStruct(activations.shape, BF16),
            jax.ShapeDtypeStruct((layers, rows, depth), BF16),
            jax.ShapeDtypeStruct((layers, rows, latents), BF16),
        ),
        in_specs=[vmem, vmem, hbm, vmem, hbm, vmem, vmem],
        out_specs=(vmem, hbm, vmem),
        scratch_shapes=[
            bf(layers, rows, depth),
            bf(*enc_weight.shape),
            bf(*dec_weight.shape),
            bf(2, layers, rb, LANES),
            f32(layers, rb, LANES),
            f32(own_rows, layers, depth),
            f32(layers, fb, latents),
            f32(1, latents),
            bf(2, layers, NEAR, 2, 2, nq, rb, LANES),
            f32(layers, rows * chunks, LANES),
            bf(layers, rows, depth),
            f32(layers, rows, latents),
            f32(layers, rows, latents),
            bf(2, layers, nf, fb, latents),
            bf(2, layers, nf, fb, latents),
            bf(layers, nf, fb, latents),
            bf(layers, nf, fb, latents),
            bf(layers, NEAR, 2, nq, rb, LANES),
            bf(layers, NEAR, 2, nq, rb, LANES),
            bf(layers, NEAR, 2, nq, rb, LANES),
            bf(layers, SLOTS, nq, rb, LANES),
            f32(layers, nq, rb, LANES),
            f32(layers, rb, LANES),
            bf(layers, nq, rb, LANES),
            bf(layers, nq, rb, LANES),
            dma((4,)),
            dma((2, layers, nq)),
            dma((2, layers, nq)),
            dma((2, layers, count)),
            dma((2, layers, count)),
            dma((2, layers, count + 1)),
            dma((2, layers, count + 1)),
            dma((2, 2, layers, nf)),
            dma((2, 2, layers, nf)),
            dma((layers, NEAR)),
            dma((layers, NEAR)),
            dma((layers, count)),
            dma((layers, count)),
            dma((layers, nq)),
            dma((layers, nq)),
        ],
        compiler_params=pltpu.CompilerParams(
            collective_id=0, has_side_effects=True, vmem_limit_bytes=63 * 2**20
        ),
    )(
        activations, targets, enc_weight, enc_bias, dec_weight, top_blocks.transpose(1, 2, 0), pair_mask,
    )
    enc_grad = jnp.einsum("lrd,lrf->ldf", a_all, pre_grad, preferred_element_type=F32)
    return recon, enc_grad


def solution(mesh):
    in_specs = (
        P("latent", None, "feature"),
        P("latent", None, "feature"),
        P(None, "feature", "latent"),
        P(None, "latent"),
        P(None, "latent", "feature"),
        P(),
        P(),
    )
    out_specs = (P("latent", None, "feature"), P(None, "feature", "latent"))
    step = functools.partial(body, mesh.shape["latent"] // 4, mesh.shape["feature"])
    return jax.shard_map(step, mesh=mesh, in_specs=in_specs, out_specs=out_specs, check_vma=False)
```

```python
import functools
import math

import jax
import jax.numpy as jnp
from jax import lax
from jax.experimental import pallas as pl
from jax.experimental.pallas import tpu as pltpu
from jax.sharding import PartitionSpec as P

BLOCK = 128
LANES = 128
F32 = jnp.float32
BF16 = jnp.bfloat16
MESH = pl.DeviceIdType.MESH
NEAR = 4
MESSAGES = (
    (1, 0, "all", 0), (1, 1, "all", 1), (-1, 0, "all", 2), (-1, 1, "all", 3),
    (2, 0, "low", 4), (2, 1, "low", 5), (-2, 0, "high", 4), (-2, 1, "high", 5),
    (0, 1, "all", 6),
)
SLOTS = 7


def kernel(
    nz, nf, scale,
    act, tgt, enc_hbm, bias, dec_hbm, top, pairs,
    recon, a_hbm, pre_out,
    a_own, enc, dec, biases, own, goal, wide_rows, mask, gate, x, xf, err_own, part, grad,
    f_out, f_in, codes, pre_own, pre_all,
    near_out, near_in, total, total_rows, far_out, far_in,
    load_sem, swap_s, swap_r, far_s, far_r, near_s, near_r,
    f_send, f_recv, g_send, g_recv, rn_s, rn_r, rf_s, rf_r,
):
    feat = lax.axis_index("feature")
    lat = lax.axis_index("latent")
    c = lat % 2
    y = (lat // 2) % 2
    z = lat // 4
    nq = nz // NEAR
    held = (z + 2) % NEAR
    offsets = [2 - nz // 2 + NEAR * j for j in range(nq)]
    own_rows = act.shape[0]
    rb = own.shape[2]
    rows, depth = a_own.shape[1:]
    chunks = depth // LANES
    latents = enc.shape[3]
    fb = 2 * rows // nf
    side = feat % 2
    group = nq * rb

    def at(zz, yy, cc):
        return {"latent": (((zz + nz) % nz) * 2 + yy) * 2 + cc}

    other_core = at(z, y, 1 - c)
    near_devices = [at(z + dz, 1 - y if dy else y, c) for dz, dy, _, _ in MESSAGES]
    far_devices = [at(z + o, y, c) for o in offsets]
    far_blocks = [((z - o + nz) % nz) // NEAR for o in offsets]
    parts = {"all": slice(0, nq), "low": slice(0, nq // 2), "high": slice(nq // 2, nq)}

    def span(which):
        s = parts[which]
        return pl.ds(s.start, s.stop - s.start)

    def peer(i):
        return (feat + i) % nf

    feature_devices = [{"feature": peer(i)} for i in range(1, nf)]
    cross_devices = [{"feature": peer(i), "latent": (z * 2 + y) * 2 + 1 - c} for i in range(1, nf)]
    everyone = [other_core] + near_devices + far_devices + feature_devices + cross_devices
    barrier = pltpu.get_barrier_semaphore()
    for device in everyone:
        pl.semaphore_signal(barrier, inc=1, device_id=device, device_id_type=MESH)
    load_enc = pltpu.make_async_copy(enc_hbm, enc.at[c], load_sem.at[0])
    load_dec = pltpu.make_async_copy(dec_hbm, dec.at[c], load_sem.at[1])
    load_enc.start()
    load_dec.start()

    def split(ref, t, put):
        values = ref[...].astype(F32)
        for k in range(chunks):
            put[t, pl.ds(k, own_rows, stride=chunks), :] = values[:, t, k * LANES:(k + 1) * LANES]

    for t in range(2):
        split(act, t, total_rows)
        own[0, t] = total_rows[t].astype(BF16)
        split(tgt, t, goal)
    local_blocks = latents // BLOCK
    place = feat // 2 * fb + lax.broadcasted_iota(jnp.int32, (fb, rows * 2), 0)
    first = ((z * 2 + y) * 2 + side) * local_blocks
    index = lax.div(place, own_rows)
    device = lax.rem(index, nq) * (4 * NEAR) + lax.div(index, nq) * 2 + c
    source = device * own_rows + lax.rem(place, own_rows)
    picked = source == lax.broadcasted_iota(jnp.int32, (fb, rows * 2), 1)
    picked = jnp.where(picked, 1.0, 0.0).astype(BF16)
    across = (((1,), (1,)), ((), ()))
    for t in range(2):
        hits = []
        for b in range(local_blocks):
            same = jnp.where(top[t] == first + b, 1.0, 0.0)
            hits.append(jnp.broadcast_to(jnp.sum(same, axis=0, keepdims=True), (BLOCK, rows * 2)))
        hits = jnp.concatenate(hits, axis=0).astype(BF16)
        mask[t] = lax.dot_general(picked, hits, across, preferred_element_type=F32)
    numbers = pairs[0].astype(F32)[1:2]
    lanes = lax.broadcasted_iota(jnp.int32, numbers.shape, 1)
    for b in range(2 * local_blocks):
        chosen = lanes == (z * 2 + y) * 2 * local_blocks + b
        value = jnp.sum(jnp.where(chosen, numbers, 0.0), axis=1, keepdims=True)
        gate[:, b * BLOCK:(b + 1) * BLOCK] = jnp.broadcast_to(value, (1, BLOCK))
    biases[c] = bias[...]
    pl.semaphore_wait(barrier, len(everyone))

    def remote(src, dst, send, recv, device):
        return pltpu.make_async_remote_copy(
            src_ref=src, dst_ref=dst, send_sem=send, recv_sem=recv, device_id=device, device_id_type=MESH
        )

    swaps = [
        remote(ref, out, swap_s.at[i], swap_r.at[i], other_core)
        for i, (ref, out) in enumerate(((bias, biases.at[c]), (enc_hbm, enc.at[c]), (dec_hbm, dec.at[c])))
    ]
    swapped = [
        remote(out, out, swap_s.at[i], swap_r.at[i], other_core)
        for i, out in enumerate((biases.at[1 - c], enc.at[1 - c], dec.at[1 - c]))
    ]

    def act_copy(t):
        return remote(a_own.at[t], a_hbm.at[t, c], swap_s.at[3 + t], swap_r.at[3 + t], other_core)

    def far_copy(g, t, j):
        ref = x.at[g, t, z % NEAR, y, z // NEAR]
        return remote(own.at[g, t], ref, far_s.at[g, t, j], far_r.at[g, t, j], far_devices[j])

    def far_arrival(g, t, j):
        ref = x.at[g, t, held, y, far_blocks[j]]
        return remote(ref, ref, far_s.at[g, t, j], far_r.at[g, t, j], far_devices[j])

    def near_copy(g, t, n):
        ref = x.at[g, t, held, y, span(MESSAGES[n][2])]
        return remote(ref, ref, near_s.at[g, t, n], near_r.at[g, t, n], near_devices[n])

    def near_arrival(g, t, n):
        dz, dy, which, _ = MESSAGES[n]
        ref = x.at[g, t, (held - dz + NEAR) % NEAR, 1 - y if dy else y, span(which)]
        return remote(ref, ref, near_s.at[g, t, n], near_r.at[g, t, n], near_devices[n])

    def gather_far(g, t):
        for j in range(nq):
            far_copy(g, t, j).start()

    def gather_near(g, t):
        for j in range(nq):
            far_arrival(g, t, j).wait_recv()
        for n in range(len(MESSAGES)):
            near_copy(g, t, n).start()

    def gather_end(g, t, out):
        for n in range(len(MESSAGES)):
            near_arrival(g, t, n).wait_recv()

        def widen(i, carry):
            blocks = x[g, t, i // 2, i % 2].astype(F32)
            xf[t, pl.ds(pl.multiple_of(i * group, 8), group), :] = blocks.reshape(group, LANES)
            return carry

        lax.fori_loop(0, 2 * NEAR, widen, 0)
        for k in range(chunks):
            out[t, :, k * LANES:(k + 1) * LANES] = xf[t, pl.ds(k, rows, stride=chunks), :].astype(BF16)

    def gather_sent(g, t):
        for j in range(nq):
            far_copy(g, t, j).wait_send()
        for n in range(len(MESSAGES)):
            near_copy(g, t, n).wait_send()

    def sum_copy(g, t, i):
        j = peer(i)
        return remote(
            f_out.at[g, t, j], f_in.at[g, t, i], f_send.at[0, g, t, i], f_recv.at[0, g, t, i], feature_devices[i - 1]
        )

    def sum_start(g, t, values):
        for j in range(nf):
            f_out[g, t, j] = values[t, j % 2, j // 2 * fb:(j // 2 + 1) * fb, :].astype(BF16)
        for i in range(1, nf):
            sum_copy(g, t, i).start()

    def sum_end(g, t, values):
        acc = values[t, side, pl.ds(pl.multiple_of(feat // 2 * fb, 8), fb), :]
        for i in range(1, nf):
            sum_copy(g, t, i).wait_recv()
            acc = acc + f_in[g, t, i].astype(F32)
        return acc

    def share_copy(t, i, mine):
        slot = codes.at[t, feat if mine else (feat - i + nf) % nf]
        return remote(slot, slot, f_send.at[1, 0, t, i], f_recv.at[1, 0, t, i], feature_devices[i - 1])

    def share_start(t):
        for i in range(1, nf):
            share_copy(t, i, True).start()

    def share_end(t):
        for i in range(1, nf):
            share_copy(t, i, False).wait_recv()

    def give_copy(t, i):
        target = {"feature": peer(i), "latent": (z * 2 + y) * 2 + side}
        return remote(
            pre_own.at[t], pre_all.at[t, c, feat // 2], g_send.at[t, i], g_recv.at[t, c, feat // 2], target
        )

    def give_start(t):
        for i in range(1, nf):
            give_copy(t, i).start()

        @pl.when(side != c)
        def _():
            give_copy(t, 0).start()

        @pl.when(side == c)
        def _():
            pre_all[t, c, feat // 2] = pre_own[t]

    def give_end(t):
        for k in range(nf // 2):
            for cc in range(2):
                slot = pre_all.at[t, cc, k]
                arrival = remote(slot, slot, g_send.at[t, 0], g_recv.at[t, cc, k], other_core)

                @pl.when(jnp.logical_not((cc == c) & (2 * k + c == feat)))
                def _():
                    arrival.wait_recv()

    def give_sent(t):
        for i in range(1, nf):
            give_copy(t, i).wait_send()

        @pl.when(side != c)
        def _():
            give_copy(t, 0).wait_send()

    def sum_sent(g, t):
        for i in range(1, nf):
            sum_copy(g, t, i).wait_send()

    def local(t, mm, yy):
        start = (mm * 2 + yy) * group
        return blocks(xf[t, pl.ds(pl.multiple_of(start, 8), group), :])

    def blocks(value):
        return value.reshape(nq, rb, LANES)

    steps = (1, -1, 2, 0)

    def rn_copy(t, n):
        dz, dy, which, slot = MESSAGES[n]
        mm = (held + dz + NEAR) % NEAR
        yy = 1 - y if dy else y
        return remote(
            near_out.at[t, mm, yy, span(which)], near_in.at[t, slot, span(which)],
            rn_s.at[t, n], rn_r.at[t, n], near_devices[n],
        )

    def reduce_near(t):
        for s, messages in enumerate(((0, 1), (2, 3), (4, 5, 6, 7), (8,))):
            mm = (held + steps[s] + NEAR) % NEAR
            for yy in ((y, 1 - y) if s < 3 else (1 - y,)):
                near_out[t, mm, yy] = local(t, mm, yy).astype(BF16)
            for n in messages:
                rn_copy(t, n).start()

    def rf_copy(t, j):
        return remote(far_out.at[t, j], far_in.at[t, j], rf_s.at[t, j], rf_r.at[t, j], far_devices[nq - 1 - j])

    def reduce_far(t):
        for n in range(len(MESSAGES)):
            rn_copy(t, n).wait_recv()
        acc = local(t, held, y)
        for slot in range(SLOTS):
            acc = acc + near_in[t, slot].astype(F32)
        total[t] = acc
        for j in range(nq):
            far_out[t, j] = total[t, far_blocks[j]].astype(BF16)
            rf_copy(t, j).start()

    def reduce_end(t):
        acc = jnp.zeros((rb, LANES), F32)
        for j in range(nq):
            rf_copy(t, j).wait_recv()
            acc = acc + far_in[t, j].astype(F32)
        own[1, t] = (acc - goal[t]).astype(BF16)
        total_rows[t] = acc

    def write_recon(t):
        for k in range(chunks):
            wide_rows[:, t, k * LANES:(k + 1) * LANES] = total_rows[t, pl.ds(k, own_rows, stride=chunks), :]

    def reduce_sent(t):
        for n in range(len(MESSAGES)):
            rn_copy(t, n).wait_send()
        for j in range(nq):
            rf_copy(t, j).wait_send()

    both = (0, 1)
    for t in both:
        gather_far(0, t)
    for copy in swaps:
        copy.start()
    for t in both:
        gather_near(0, t)
    load_enc.wait()
    for copy in swapped[:2]:
        copy.wait_recv()
    for t in both:
        gather_end(0, t, a_own)
        for cc in range(2):
            part[t, cc] = jnp.dot(a_own[t], enc[cc, t], preferred_element_type=F32)
        sum_start(0, t, part)
    store_act = [pltpu.make_async_copy(a_own.at[t], a_hbm.at[t, c], load_sem.at[2 + t]) for t in both]
    for t in both:
        store_act[t].start()
        act_copy(t).start()
        value = sum_end(0, t, part) + biases[side, t:t + 1, :]
        codes[t, feat] = (mask[t] * value).astype(BF16)
        share_start(t)
    load_dec.wait()
    swapped[2].wait_recv()

    def whole(t, cc):
        mine = [codes[t, 2 * k + cc].astype(F32) for k in range(nf // 2)]
        return jnp.concatenate(mine, axis=0)

    wide = 2 * LANES
    for t in both:
        share_end(t)
        terms = []
        for cc in range(2):
            if t == 0:
                terms.append((whole(0, cc).astype(BF16), cc, 0))
            else:
                lanes = slice(cc * latents, (cc + 1) * latents)
                terms.append(((whole(0, cc) * gate[:, lanes]).astype(BF16), cc, 1))
                terms.append((whole(1, cc).astype(BF16), cc, 2))
        for n in range(depth // wide):
            cols = slice(n * wide, (n + 1) * wide)
            value = sum(jnp.dot(code, dec[cc, p, :, cols], preferred_element_type=F32) for code, cc, p in terms)
            for k in range(2):
                xf[t, pl.ds(2 * n + k, rows, stride=chunks), :] = value[:, k * LANES:(k + 1) * LANES]
        reduce_near(t)
    for copy in swaps:
        copy.wait_send()
    for t in both:
        gather_sent(0, t)
        sum_sent(0, t)
        for i in range(1, nf):
            share_copy(t, i, True).wait_send()
    for t in both:
        reduce_far(t)
    for t in both:
        reduce_end(t)
        gather_far(1, t)
    for t in both:
        gather_near(1, t)
    for t in both:
        reduce_sent(t)
        write_recon(t)
    recon[...] = wide_rows[...].astype(BF16)

    def gradient(t, cc, p):
        return lax.dot_general(err_own[t], dec[cc, p], across, preferred_element_type=F32)

    gather_end(1, 0, err_own)
    for cc in range(2):
        grad[0, cc] = gradient(0, cc, 0)
    gather_end(1, 1, err_own)
    for cc in range(2):
        grad[1, cc] = gradient(1, cc, 2)
    sum_start(1, 1, grad)
    for cc in range(2):
        grad[0, cc] = grad[0, cc] + gate[:, cc * latents:(cc + 1) * latents] * gradient(1, cc, 1)
    sum_start(1, 0, grad)
    for t in (1, 0):
        pre_own[t] = (mask[t] * sum_end(1, t, grad) * scale).astype(BF16)
        give_start(t)
    for t in both:
        gather_sent(1, t)
        sum_sent(1, t)
        store_act[t].wait()
        act_copy(t).wait_send()
        arrived = a_hbm.at[t, 1 - c]
        remote(arrived, arrived, swap_s.at[3 + t], swap_r.at[3 + t], other_core).wait_recv()
    for t in (1, 0):
        give_end(t)
        for cc in range(2):
            whole_rows = jnp.concatenate([pre_all[t, cc, k].astype(F32) for k in range(nf // 2)], axis=0)
            pre_out[t, cc] = whole_rows.astype(BF16)
    for t in both:
        give_sent(t)


def body(nz, nf, activations, targets, enc_weight, enc_bias, dec_weight, top_blocks, pair_mask):
    own_rows, layers, depth = activations.shape
    all_rows = top_blocks.shape[0]
    rows = all_rows // 2
    latents = enc_weight.shape[2]
    chunks = depth // LANES
    rb = own_rows * chunks
    fb = all_rows // nf
    nq = nz // NEAR
    vmem = pl.BlockSpec(memory_space=pltpu.VMEM)
    hbm = pl.BlockSpec(memory_space=pltpu.HBM)
    dma = pltpu.SemaphoreType.DMA
    bf, f32 = (lambda *s: pltpu.VMEM(s, BF16)), (lambda *s: pltpu.VMEM(s, F32))
    count = len(MESSAGES)
    recon, a_all, pre_grad = pl.pallas_call(
        functools.partial(kernel, nz, nf, 1.0 / math.sqrt(all_rows)),
        out_shape=(
            jax.ShapeDtypeStruct(activations.shape, BF16),
            jax.ShapeDtypeStruct((layers, 2, rows, depth), BF16),
            jax.ShapeDtypeStruct((layers, 2, rows, latents), BF16),
        ),
        in_specs=[vmem, vmem, hbm, vmem, hbm, vmem, vmem],
        out_specs=(vmem, hbm, vmem),
        scratch_shapes=[
            bf(layers, rows, depth),
            bf(2, *enc_weight.shape),
            bf(2, *dec_weight.shape),
            f32(2, *enc_bias.shape),
            bf(2, layers, rb, LANES),
            f32(layers, rb, LANES),
            f32(own_rows, layers, depth),
            f32(layers, fb, latents),
            f32(1, 2 * latents),
            bf(2, layers, NEAR, 2, nq, rb, LANES),
            f32(layers, rows * chunks, LANES),
            bf(layers, rows, depth),
            f32(layers, 2, rows, latents),
            f32(layers, 2, rows, latents),
            bf(2, layers, nf, fb, latents),
            bf(2, layers, nf, fb, latents),
            bf(layers, nf, fb, latents),
            bf(layers, fb, latents),
            bf(layers, 2, nf // 2, fb, latents),
            bf(layers, NEAR, 2, nq, rb, LANES),
            bf(layers, SLOTS, nq, rb, LANES),
            f32(layers, nq, rb, LANES),
            f32(layers, rb, LANES),
            bf(layers, nq, rb, LANES),
            bf(layers, nq, rb, LANES),
            dma((4,)),
            dma((5,)),
            dma((5,)),
            dma((2, layers, nq)),
            dma((2, layers, nq)),
            dma((2, layers, count)),
            dma((2, layers, count)),
            dma((2, 2, layers, nf)),
            dma((2, 2, layers, nf)),
            dma((layers, nf)),
            dma((layers, 2, nf // 2)),
            dma((layers, count)),
            dma((layers, count)),
            dma((layers, nq)),
            dma((layers, nq)),
        ],
        compiler_params=pltpu.CompilerParams(
            collective_id=0, has_side_effects=True, vmem_limit_bytes=63 * 2**20
        ),
    )(
        activations, targets, enc_weight, enc_bias, dec_weight, top_blocks.transpose(1, 2, 0), pair_mask,
    )
    enc_grad = jnp.einsum(
        "lrd,lrf->ldf",
        a_all.reshape(layers, all_rows, depth),
        pre_grad.reshape(layers, all_rows, latents),
        preferred_element_type=F32,
    )
    return recon, enc_grad


def solution(mesh):
    in_specs = (
        P("latent", None, "feature"),
        P("latent", None, "feature"),
        P(None, "feature", "latent"),
        P(None, "latent"),
        P(None, "latent", "feature"),
        P(),
        P(),
    )
    out_specs = (P("latent", None, "feature"), P(None, "feature", "latent"))
    step = functools.partial(body, mesh.shape["latent"] // 4, mesh.shape["feature"])
    return jax.shard_map(step, mesh=mesh, in_specs=in_specs, out_specs=out_specs, check_vma=False)
```

```python
import functools
import math

import jax
import jax.numpy as jnp
from jax import lax
from jax.experimental import pallas as pl
from jax.experimental.pallas import tpu as pltpu
from jax.sharding import PartitionSpec as P

BLOCK = 128
LANES = 128
F32 = jnp.float32
BF16 = jnp.bfloat16
MESH = pl.DeviceIdType.MESH
NEAR = 4
MESSAGES = (
    (2, 1, "low", 5), (-2, 1, "high", 5), (1, 1, "all", 1), (-1, 1, "all", 3),
    (2, 0, "low", 4), (-2, 0, "high", 4), (0, 1, "all", 6), (1, 0, "all", 0), (-1, 0, "all", 2),
)
ARRIVALS = (7, 8, 4, 5, 6, 2, 3, 0, 1)
SLOTS = 7


def kernel(
    nz, nf, scale,
    act_hbm, tgt_hbm, enc_hbm, bias_hbm, dec_hbm, top_hbm, pairs_hbm,
    recon_hbm, a_hbm, pre_hbm,
    act, tgt, bias, top, pairs, recon, pre_out, a_own, enc, dec, biases, own, goal, wide_rows, mask, gate, x, xf, err_own, part, grad,
    f_out, f_in, codes, pre_own, pre_all,
    near_out, near_in, total, total_rows, far_out, far_in,
    load_sem, small_sem, swap_s, swap_r, far_s, far_r, near_s, near_r,
    f_send, f_recv, g_send, g_recv, rn_s, rn_r, rf_s, rf_r,
):
    feat = lax.axis_index("feature")
    lat = lax.axis_index("latent")
    c = lat % 2
    y = (lat // 2) % 2
    z = lat // 4
    nq = nz // NEAR
    held = (z + 2) % NEAR
    offsets = [2 - nz // 2 + NEAR * j for j in range(nq)]
    own_rows = act.shape[0]
    inputs = ((act_hbm, act), (tgt_hbm, tgt), (bias_hbm, bias), (top_hbm, top), (pairs_hbm, pairs))
    loads = [pltpu.make_async_copy(a, b, small_sem.at[i]) for i, (a, b) in enumerate(inputs)]
    rb = own.shape[2]
    rows, depth = a_own.shape[1:]
    chunks = depth // LANES
    latents = enc.shape[3]
    fb = 2 * rows // nf
    side = feat % 2
    group = nq * rb

    def at(zz, yy, cc):
        return {"latent": (((zz + nz) % nz) * 2 + yy) * 2 + cc}

    other_core = at(z, y, 1 - c)
    near_devices = [at(z + dz, 1 - y if dy else y, c) for dz, dy, _, _ in MESSAGES]
    far_devices = [at(z + o, y, c) for o in offsets]
    far_blocks = [((z - o + nz) % nz) // NEAR for o in offsets]
    parts = {"all": slice(0, nq), "low": slice(0, nq // 2), "high": slice(nq // 2, nq)}

    def span(which):
        s = parts[which]
        return pl.ds(s.start, s.stop - s.start)

    relations = [(0, 0)] + [(a, b) for a, b in ((1, 2), (0, 2), (1, 1), (1, 3), (0, 1), (0, 3), (1, 0))]

    def peer(i):
        a, b = relations[i]
        return (feat // 4 + a) % 2 * 4 + (feat % 4 + b) % 4

    def giver(i):
        a, b = relations[i]
        return (feat // 4 + a) % 2 * 4 + (feat % 4 + 4 - b) % 4

    feature_devices = [{"feature": peer(i)} for i in range(1, nf)]
    cross_devices = [{"feature": peer(i), "latent": (z * 2 + y) * 2 + 1 - c} for i in range(1, nf)]
    everyone = [other_core] + near_devices + far_devices + feature_devices + cross_devices
    barrier = pltpu.get_barrier_semaphore()
    for device in everyone:
        pl.semaphore_signal(barrier, inc=1, device_id=device, device_id_type=MESH)
    for copy in loads:
        copy.start()
    load_enc = pltpu.make_async_copy(enc_hbm, enc.at[c], load_sem.at[0])
    load_dec = pltpu.make_async_copy(dec_hbm, dec.at[c], load_sem.at[1])
    load_enc.start()
    load_dec.start()

    for copy in loads:
        copy.wait()

    def split(ref, t, put):
        values = ref[...].astype(F32)
        for k in range(chunks):
            put[t, pl.ds(k, own_rows, stride=chunks), :] = values[:, t, k * LANES:(k + 1) * LANES]

    for t in range(2):
        split(act, t, total_rows)
        own[0, t] = total_rows[t].astype(BF16)
        split(tgt, t, goal)
    local_blocks = latents // BLOCK
    place = feat // 2 * fb + lax.broadcasted_iota(jnp.int32, (fb, rows * 2), 0)
    first = ((z * 2 + y) * 2 + side) * local_blocks
    index = lax.div(place, own_rows)
    device = lax.rem(index, nq) * (4 * NEAR) + lax.div(index, nq) * 2 + c
    source = device * own_rows + lax.rem(place, own_rows)
    picked = source == lax.broadcasted_iota(jnp.int32, (fb, rows * 2), 1)
    picked = jnp.where(picked, 1.0, 0.0).astype(BF16)
    across = (((1,), (1,)), ((), ()))
    for t in range(2):
        hits = []
        for b in range(local_blocks):
            same = jnp.where(top[t] == first + b, 1.0, 0.0)
            hits.append(jnp.broadcast_to(jnp.sum(same, axis=0, keepdims=True), (BLOCK, rows * 2)))
        hits = jnp.concatenate(hits, axis=0).astype(BF16)
        mask[t] = lax.dot_general(picked, hits, across, preferred_element_type=F32)
    numbers = pairs[0].astype(F32)[1:2]
    lanes = lax.broadcasted_iota(jnp.int32, numbers.shape, 1)
    for b in range(2 * local_blocks):
        chosen = lanes == (z * 2 + y) * 2 * local_blocks + b
        value = jnp.sum(jnp.where(chosen, numbers, 0.0), axis=1, keepdims=True)
        gate[:, b * BLOCK:(b + 1) * BLOCK] = jnp.broadcast_to(value, (1, BLOCK))
    biases[c] = bias[...]
    pl.semaphore_wait(barrier, len(everyone))

    def remote(src, dst, send, recv, device):
        return pltpu.make_async_remote_copy(
            src_ref=src, dst_ref=dst, send_sem=send, recv_sem=recv, device_id=device, device_id_type=MESH
        )

    swaps = [
        remote(ref, out, swap_s.at[i], swap_r.at[i], other_core)
        for i, (ref, out) in enumerate(((bias, biases.at[c]), (enc_hbm, enc.at[c]), (dec_hbm, dec.at[c])))
    ]
    swapped = [
        remote(out, out, swap_s.at[i], swap_r.at[i], other_core)
        for i, out in enumerate((biases.at[1 - c], enc.at[1 - c], dec.at[1 - c]))
    ]

    def act_copy(t):
        return remote(a_own.at[t], a_hbm.at[t, c], swap_s.at[3 + t], swap_r.at[3 + t], other_core)

    def far_copy(g, t, j):
        ref = x.at[g, t, z % NEAR, y, z // NEAR]
        return remote(own.at[g, t], ref, far_s.at[g, t, j], far_r.at[g, t, j], far_devices[j])

    def far_arrival(g, t, j):
        ref = x.at[g, t, held, y, far_blocks[j]]
        return remote(ref, ref, far_s.at[g, t, j], far_r.at[g, t, j], far_devices[j])

    def near_copy(g, t, n):
        ref = x.at[g, t, held, y, span(MESSAGES[n][2])]
        return remote(ref, ref, near_s.at[g, t, n], near_r.at[g, t, n], near_devices[n])

    def near_arrival(g, t, n):
        dz, dy, which, _ = MESSAGES[n]
        ref = x.at[g, t, (held - dz + NEAR) % NEAR, 1 - y if dy else y, span(which)]
        return remote(ref, ref, near_s.at[g, t, n], near_r.at[g, t, n], near_devices[n])

    def gather_far(g, t):
        for j in range(nq):
            far_copy(g, t, j).start()

    def gather_near(g, t):
        for j in range(nq):
            far_arrival(g, t, j).wait_recv()
        for n in range(len(MESSAGES)):
            near_copy(g, t, n).start()

    def gather_end(g, t, out):
        def widen(mm, yy, which):
            piece = parts[which]
            count = (piece.stop - piece.start) * rb
            start = ((mm * 2 + yy) * nq + piece.start) * rb
            values = x[g, t, mm, yy, span(which)].astype(F32).reshape(count, LANES)
            xf[t, pl.ds(pl.multiple_of(start, 8), count), :] = values

        widen(held, y, "all")
        for n in ARRIVALS:
            dz, dy, which, _ = MESSAGES[n]
            near_arrival(g, t, n).wait_recv()
            widen((held - dz + NEAR) % NEAR, 1 - y if dy else y, which)
        for k in range(chunks):
            out[t, :, k * LANES:(k + 1) * LANES] = xf[t, pl.ds(k, rows, stride=chunks), :].astype(BF16)

    def gather_sent(g, t):
        for j in range(nq):
            far_copy(g, t, j).wait_send()
        for n in range(len(MESSAGES)):
            near_copy(g, t, n).wait_send()

    def sum_copy(g, t, i):
        j = peer(i)
        return remote(
            f_out.at[g, t, j], f_in.at[g, t, i], f_send.at[0, g, t, i], f_recv.at[0, g, t, i], feature_devices[i - 1]
        )

    def sum_start(g, t, values):
        for j in range(nf):
            f_out[g, t, j] = values[t, j % 2, j // 2 * fb:(j // 2 + 1) * fb, :].astype(BF16)
        for i in range(1, nf):
            sum_copy(g, t, i).start()

    def sum_end(g, t, values):
        acc = values[t, side, pl.ds(pl.multiple_of(feat // 2 * fb, 8), fb), :]
        for i in range(1, nf):
            sum_copy(g, t, i).wait_recv()
            acc = acc + f_in[g, t, i].astype(F32)
        return acc

    def share_copy(t, i, mine):
        slot = codes.at[t, feat if mine else giver(i)]
        return remote(slot, slot, f_send.at[1, 0, t, i], f_recv.at[1, 0, t, i], feature_devices[i - 1])

    def share_start(t):
        for i in range(1, nf):
            share_copy(t, i, True).start()

    def share_end(t):
        for i in range(1, nf):
            share_copy(t, i, False).wait_recv()

    def give_copy(t, i):
        target = {"feature": peer(i), "latent": (z * 2 + y) * 2 + side}
        return remote(
            pre_own.at[t], pre_all.at[t, c, feat // 2], g_send.at[t, i], g_recv.at[t, c, feat // 2], target
        )

    def give_start(t):
        for i in range(1, nf):
            give_copy(t, i).start()

        @pl.when(side != c)
        def _():
            give_copy(t, 0).start()

        @pl.when(side == c)
        def _():
            pre_all[t, c, feat // 2] = pre_own[t]

    def give_end(t):
        for k in range(nf // 2):
            for cc in range(2):
                slot = pre_all.at[t, cc, k]
                arrival = remote(slot, slot, g_send.at[t, 0], g_recv.at[t, cc, k], other_core)

                @pl.when(jnp.logical_not((cc == c) & (2 * k + c == feat)))
                def _():
                    arrival.wait_recv()

    def give_sent(t):
        for i in range(1, nf):
            give_copy(t, i).wait_send()

        @pl.when(side != c)
        def _():
            give_copy(t, 0).wait_send()

    def sum_sent(g, t):
        for i in range(1, nf):
            sum_copy(g, t, i).wait_send()

    def local(t, mm, yy):
        start = (mm * 2 + yy) * group
        return blocks(xf[t, pl.ds(pl.multiple_of(start, 8), group), :])

    def blocks(value):
        return value.reshape(nq, rb, LANES)

    def rn_copy(t, n):
        dz, dy, which, slot = MESSAGES[n]
        mm = (held + dz + NEAR) % NEAR
        yy = 1 - y if dy else y
        return remote(
            near_out.at[t, mm, yy, span(which)], near_in.at[t, slot, span(which)],
            rn_s.at[t, n], rn_r.at[t, n], near_devices[n],
        )

    def reduce_near(t):
        for n, (dz, dy, which, _) in enumerate(MESSAGES):
            if which != "high":
                mm = (held + dz + NEAR) % NEAR
                yy = 1 - y if dy else y
                near_out[t, mm, yy] = local(t, mm, yy).astype(BF16)
            rn_copy(t, n).start()

    def rf_copy(t, j):
        return remote(far_out.at[t, j], far_in.at[t, j], rf_s.at[t, j], rf_r.at[t, j], far_devices[nq - 1 - j])

    def reduce_far(t):
        for n in range(len(MESSAGES)):
            rn_copy(t, n).wait_recv()
        acc = local(t, held, y)
        for slot in range(SLOTS):
            acc = acc + near_in[t, slot].astype(F32)
        total[t] = acc
        for j in range(nq):
            far_out[t, j] = total[t, far_blocks[j]].astype(BF16)
            rf_copy(t, j).start()

    def reduce_end(t):
        acc = jnp.zeros((rb, LANES), F32)
        for j in range(nq):
            rf_copy(t, j).wait_recv()
            acc = acc + far_in[t, j].astype(F32)
        own[1, t] = (acc - goal[t]).astype(BF16)
        total_rows[t] = acc

    def write_recon(t):
        for k in range(chunks):
            wide_rows[:, t, k * LANES:(k + 1) * LANES] = total_rows[t, pl.ds(k, own_rows, stride=chunks), :]

    def reduce_sent(t):
        for n in range(len(MESSAGES)):
            rn_copy(t, n).wait_send()
        for j in range(nq):
            rf_copy(t, j).wait_send()

    both = (0, 1)
    for t in both:
        gather_far(0, t)
    for copy in swaps:
        copy.start()
    for t in both:
        gather_near(0, t)
    load_enc.wait()
    for copy in swapped[:2]:
        copy.wait_recv()
    for t in both:
        gather_end(0, t, a_own)
        for cc in range(2):
            part[t, cc] = jnp.dot(a_own[t], enc[cc, t], preferred_element_type=F32)
        sum_start(0, t, part)
    store_act = [pltpu.make_async_copy(a_own.at[t], a_hbm.at[t, c], load_sem.at[2 + t]) for t in both]
    for t in both:
        store_act[t].start()
        act_copy(t).start()
        value = sum_end(0, t, part) + biases[side, t:t + 1, :]
        codes[t, feat] = (mask[t] * value).astype(BF16)
        share_start(t)
    load_dec.wait()
    swapped[2].wait_recv()

    def whole(t, cc):
        mine = [codes[t, 2 * k + cc].astype(F32) for k in range(nf // 2)]
        return jnp.concatenate(mine, axis=0)

    wide = 2 * LANES
    for t in both:
        share_end(t)
        terms = []
        for cc in range(2):
            if t == 0:
                terms.append((whole(0, cc).astype(BF16), cc, 0))
            else:
                lanes = slice(cc * latents, (cc + 1) * latents)
                terms.append(((whole(0, cc) * gate[:, lanes]).astype(BF16), cc, 1))
                terms.append((whole(1, cc).astype(BF16), cc, 2))
        for n in range(depth // wide):
            cols = slice(n * wide, (n + 1) * wide)
            value = sum(jnp.dot(code, dec[cc, p, :, cols], preferred_element_type=F32) for code, cc, p in terms)
            for k in range(2):
                xf[t, pl.ds(2 * n + k, rows, stride=chunks), :] = value[:, k * LANES:(k + 1) * LANES]
        reduce_near(t)
    for copy in swaps:
        copy.wait_send()
    for t in both:
        gather_sent(0, t)
        sum_sent(0, t)
        for i in range(1, nf):
            share_copy(t, i, True).wait_send()
    for t in both:
        reduce_far(t)
    for t in both:
        reduce_end(t)
        gather_far(1, t)
    for t in both:
        gather_near(1, t)
    for t in both:
        reduce_sent(t)
        write_recon(t)
    recon[...] = wide_rows[...].astype(BF16)
    store_recon = pltpu.make_async_copy(recon, recon_hbm, small_sem.at[0])
    store_recon.start()

    def gradient(t, cc, p):
        return lax.dot_general(err_own[t], dec[cc, p], across, preferred_element_type=F32)

    gather_end(1, 0, err_own)
    for cc in range(2):
        grad[0, cc] = gradient(0, cc, 0)
    gather_end(1, 1, err_own)
    for cc in range(2):
        grad[1, cc] = gradient(1, cc, 2)
    sum_start(1, 1, grad)
    for cc in range(2):
        grad[0, cc] = grad[0, cc] + gate[:, cc * latents:(cc + 1) * latents] * gradient(1, cc, 1)
    sum_start(1, 0, grad)
    for t in (1, 0):
        pre_own[t] = (mask[t] * sum_end(1, t, grad) * scale).astype(BF16)
        give_start(t)
    for t in both:
        gather_sent(1, t)
        sum_sent(1, t)
        store_act[t].wait()
        act_copy(t).wait_send()
        arrived = a_hbm.at[t, 1 - c]
        remote(arrived, arrived, swap_s.at[3 + t], swap_r.at[3 + t], other_core).wait_recv()
    store_pre = [pltpu.make_async_copy(pre_out.at[t], pre_hbm.at[t], small_sem.at[1 + t]) for t in both]
    for t in (1, 0):
        give_end(t)
        for cc in range(2):
            whole_rows = jnp.concatenate([pre_all[t, cc, k].astype(F32) for k in range(nf // 2)], axis=0)
            pre_out[t, cc] = whole_rows.astype(BF16)
        store_pre[t].start()
    store_recon.wait()
    for t in both:
        give_sent(t)
        store_pre[t].wait()


def body(nz, nf, activations, targets, enc_weight, enc_bias, dec_weight, top_blocks, pair_mask):
    own_rows, layers, depth = activations.shape
    all_rows = top_blocks.shape[0]
    rows = all_rows // 2
    latents = enc_weight.shape[2]
    chunks = depth // LANES
    rb = own_rows * chunks
    fb = all_rows // nf
    nq = nz // NEAR
    hbm = pl.BlockSpec(memory_space=pltpu.HBM)
    dma = pltpu.SemaphoreType.DMA
    bf, f32 = (lambda *s: pltpu.VMEM(s, BF16)), (lambda *s: pltpu.VMEM(s, F32))
    count = len(MESSAGES)
    recon, a_all, pre_grad = pl.pallas_call(
        functools.partial(kernel, nz, nf, 1.0 / math.sqrt(all_rows)),
        out_shape=(
            jax.ShapeDtypeStruct(activations.shape, BF16),
            jax.ShapeDtypeStruct((layers, 2, rows, depth), BF16),
            jax.ShapeDtypeStruct((layers, 2, rows, latents), BF16),
        ),
        in_specs=[hbm] * 7,
        out_specs=(hbm, hbm, hbm),
        scratch_shapes=[
            bf(*activations.shape),
            bf(*targets.shape),
            f32(*enc_bias.shape),
            pltpu.VMEM((layers, top_blocks.shape[2], all_rows), jnp.int32),
            pltpu.VMEM(pair_mask.shape, jnp.int32),
            bf(*activations.shape),
            bf(layers, 2, rows, latents),
            bf(layers, rows, depth),
            bf(2, *enc_weight.shape),
            bf(2, *dec_weight.shape),
            f32(2, *enc_bias.shape),
            bf(2, layers, rb, LANES),
            f32(layers, rb, LANES),
            f32(own_rows, layers, depth),
            f32(layers, fb, latents),
            f32(1, 2 * latents),
            bf(2, layers, NEAR, 2, nq, rb, LANES),
            f32(layers, rows * chunks, LANES),
            bf(layers, rows, depth),
            f32(layers, 2, rows, latents),
            f32(layers, 2, rows, latents),
            bf(2, layers, nf, fb, latents),
            bf(2, layers, nf, fb, latents),
            bf(layers, nf, fb, latents),
            bf(layers, fb, latents),
            bf(layers, 2, nf // 2, fb, latents),
            bf(layers, NEAR, 2, nq, rb, LANES),
            bf(layers, SLOTS, nq, rb, LANES),
            f32(layers, nq, rb, LANES),
            f32(layers, rb, LANES),
            bf(layers, nq, rb, LANES),
            bf(layers, nq, rb, LANES),
            dma((4,)),
            dma((5,)),
            dma((5,)),
            dma((5,)),
            dma((2, layers, nq)),
            dma((2, layers, nq)),
            dma((2, layers, count)),
            dma((2, layers, count)),
            dma((2, 2, layers, nf)),
            dma((2, 2, layers, nf)),
            dma((layers, nf)),
            dma((layers, 2, nf // 2)),
            dma((layers, count)),
            dma((layers, count)),
            dma((layers, nq)),
            dma((layers, nq)),
        ],
        compiler_params=pltpu.CompilerParams(
            collective_id=0, has_side_effects=True, vmem_limit_bytes=63 * 2**20
        ),
    )(
        activations, targets, enc_weight, enc_bias, dec_weight, top_blocks.transpose(1, 2, 0), pair_mask,
    )
    enc_grad = jnp.einsum(
        "lrd,lrf->ldf",
        a_all.reshape(layers, all_rows, depth),
        pre_grad.reshape(layers, all_rows, latents),
        preferred_element_type=F32,
    )
    return recon, enc_grad


def solution(mesh):
    in_specs = (
        P("latent", None, "feature"),
        P("latent", None, "feature"),
        P(None, "feature", "latent"),
        P(None, "latent"),
        P(None, "latent", "feature"),
        P(),
        P(),
    )
    out_specs = (P("latent", None, "feature"), P(None, "feature", "latent"))
    step = functools.partial(body, mesh.shape["latent"] // 4, mesh.shape["feature"])
    return jax.shard_map(step, mesh=mesh, in_specs=in_specs, out_specs=out_specs, check_vma=False)
```

```python
import functools
import math

import jax
import jax.numpy as jnp
from jax import lax
from jax.experimental import pallas as pl
from jax.experimental.pallas import tpu as pltpu
from jax.sharding import PartitionSpec as P

BLOCK = 128
LANES = 128
F32 = jnp.float32
BF16 = jnp.bfloat16
MESH = pl.DeviceIdType.MESH
NEAR = 4
MESSAGES = (
    (2, 1, "low", 5), (-2, 1, "high", 5), (1, 1, "all", 1), (-1, 1, "all", 3),
    (2, 0, "low", 4), (-2, 0, "high", 4), (0, 1, "all", 6), (1, 0, "all", 0), (-1, 0, "all", 2),
)
ARRIVALS = (7, 8, 4, 5, 6, 2, 3, 0, 1)
SLOTS = 7


def kernel(
    nz, nf, scale,
    act_hbm, tgt_hbm, enc_hbm, bias_hbm, dec_hbm, top_hbm, pairs_hbm,
    recon_hbm, a_hbm, pre_hbm,
    act, tgt, bias, top, pairs, recon, pre_out, a_own, enc, dec, biases, own, goal, wide_rows, mask, gate, x, xf, err_own, part, grad,
    f_out, f_in, codes, pre_own, pre_all,
    near_out, near_in, total, total_rows, far_out, far_in,
    load_sem, small_sem, swap_s, swap_r, far_s, far_r, near_s, near_r,
    f_send, f_recv, g_send, g_recv, rn_s, rn_r, rf_s, rf_r,
):
    feat = lax.axis_index("feature")
    lat = lax.axis_index("latent")
    c = lat % 2
    y = (lat // 2) % 2
    z = lat // 4
    nq = nz // NEAR
    held = (z + 2) % NEAR
    offsets = [2 - nz // 2 + NEAR * j for j in range(nq)]
    own_rows = act.shape[0]
    inputs = ((act_hbm, act), (tgt_hbm, tgt), (bias_hbm, bias), (top_hbm, top), (pairs_hbm, pairs))
    loads = [pltpu.make_async_copy(a, b, small_sem.at[i]) for i, (a, b) in enumerate(inputs)]
    rb = own.shape[2]
    rows, depth = a_own.shape[1:]
    chunks = depth // LANES
    latents = enc.shape[3]
    fb = 2 * rows // nf
    side = feat % 2
    group = nq * rb

    def at(zz, yy, cc):
        return {"latent": (((zz + nz) % nz) * 2 + yy) * 2 + cc}

    other_core = at(z, y, 1 - c)
    near_devices = [at(z + dz, 1 - y if dy else y, c) for dz, dy, _, _ in MESSAGES]
    far_devices = [at(z + o, y, c) for o in offsets]
    far_order = sorted(range(nq), key=lambda j: -abs(offsets[j]))
    far_blocks = [((z - o + nz) % nz) // NEAR for o in offsets]
    parts = {"all": slice(0, nq), "low": slice(0, nq // 2), "high": slice(nq // 2, nq)}

    def span(which):
        s = parts[which]
        return pl.ds(s.start, s.stop - s.start)

    relations = [(0, 0)] + [(a, b) for a, b in ((1, 2), (0, 2), (1, 1), (1, 3), (0, 1), (0, 3), (1, 0))]

    def peer(i):
        a, b = relations[i]
        return (feat // 4 + a) % 2 * 4 + (feat % 4 + b) % 4

    def giver(i):
        a, b = relations[i]
        return (feat // 4 + a) % 2 * 4 + (feat % 4 + 4 - b) % 4

    feature_devices = [{"feature": peer(i)} for i in range(1, nf)]
    cross_devices = [{"feature": peer(i), "latent": (z * 2 + y) * 2 + 1 - c} for i in range(1, nf)]
    everyone = [far_devices[j] for j in far_order] + cross_devices + feature_devices + near_devices + [other_core]
    barrier = pltpu.get_barrier_semaphore()
    for device in everyone:
        pl.semaphore_signal(barrier, inc=1, device_id=device, device_id_type=MESH)
    for copy in loads:
        copy.start()
    load_enc = pltpu.make_async_copy(enc_hbm, enc.at[c], load_sem.at[0])
    load_dec = pltpu.make_async_copy(dec_hbm, dec.at[c], load_sem.at[1])
    load_enc.start()
    load_dec.start()

    for copy in loads:
        copy.wait()

    def split(ref, t, put):
        values = ref[...].astype(F32)
        for k in range(chunks):
            put[t, pl.ds(k, own_rows, stride=chunks), :] = values[:, t, k * LANES:(k + 1) * LANES]

    for t in range(2):
        split(act, t, total_rows)
        own[0, t] = total_rows[t].astype(BF16)
        split(tgt, t, goal)
    local_blocks = latents // BLOCK
    place = feat // 2 * fb + lax.broadcasted_iota(jnp.int32, (fb, rows * 2), 0)
    first = ((z * 2 + y) * 2 + side) * local_blocks
    index = lax.div(place, own_rows)
    device = lax.rem(index, nq) * (4 * NEAR) + lax.div(index, nq) * 2 + c
    source = device * own_rows + lax.rem(place, own_rows)
    picked = source == lax.broadcasted_iota(jnp.int32, (fb, rows * 2), 1)
    picked = jnp.where(picked, 1.0, 0.0).astype(BF16)
    across = (((1,), (1,)), ((), ()))
    for t in range(2):
        hits = []
        for b in range(local_blocks):
            same = jnp.where(top[t] == first + b, 1.0, 0.0)
            hits.append(jnp.broadcast_to(jnp.sum(same, axis=0, keepdims=True), (BLOCK, rows * 2)))
        hits = jnp.concatenate(hits, axis=0).astype(BF16)
        mask[t] = lax.dot_general(picked, hits, across, preferred_element_type=F32)
    numbers = pairs[0].astype(F32)[1:2]
    lanes = lax.broadcasted_iota(jnp.int32, numbers.shape, 1)
    for b in range(2 * local_blocks):
        chosen = lanes == (z * 2 + y) * 2 * local_blocks + b
        value = jnp.sum(jnp.where(chosen, numbers, 0.0), axis=1, keepdims=True)
        gate[:, b * BLOCK:(b + 1) * BLOCK] = jnp.broadcast_to(value, (1, BLOCK))
    biases[c] = bias[...]
    pl.semaphore_wait(barrier, len(everyone))

    def remote(src, dst, send, recv, device):
        return pltpu.make_async_remote_copy(
            src_ref=src, dst_ref=dst, send_sem=send, recv_sem=recv, device_id=device, device_id_type=MESH
        )

    swaps = [
        remote(ref, out, swap_s.at[i], swap_r.at[i], other_core)
        for i, (ref, out) in enumerate(((bias, biases.at[c]), (enc_hbm, enc.at[c]), (dec_hbm, dec.at[c])))
    ]
    swapped = [
        remote(out, out, swap_s.at[i], swap_r.at[i], other_core)
        for i, out in enumerate((biases.at[1 - c], enc.at[1 - c], dec.at[1 - c]))
    ]

    def act_copy(t):
        return remote(a_own.at[t], a_hbm.at[t, c], swap_s.at[3 + t], swap_r.at[3 + t], other_core)

    def far_copy(g, t, j):
        ref = x.at[g, t, z % NEAR, y, z // NEAR]
        return remote(own.at[g, t], ref, far_s.at[g, t, j], far_r.at[g, t, j], far_devices[j])

    def far_arrival(g, t, j):
        ref = x.at[g, t, held, y, far_blocks[j]]
        return remote(ref, ref, far_s.at[g, t, j], far_r.at[g, t, j], far_devices[j])

    def near_copy(g, t, n):
        ref = x.at[g, t, held, y, span(MESSAGES[n][2])]
        return remote(ref, ref, near_s.at[g, t, n], near_r.at[g, t, n], near_devices[n])

    def near_arrival(g, t, n):
        dz, dy, which, _ = MESSAGES[n]
        ref = x.at[g, t, (held - dz + NEAR) % NEAR, 1 - y if dy else y, span(which)]
        return remote(ref, ref, near_s.at[g, t, n], near_r.at[g, t, n], near_devices[n])

    def gather_far(g, t):
        for j in far_order:
            far_copy(g, t, j).start()

    def gather_near(g, t):
        for j in range(nq):
            far_arrival(g, t, j).wait_recv()
        for n in range(len(MESSAGES)):
            near_copy(g, t, n).start()

    def gather_end(g, t, out):
        def widen(mm, yy, which):
            piece = parts[which]
            count = (piece.stop - piece.start) * rb
            start = ((mm * 2 + yy) * nq + piece.start) * rb
            values = x[g, t, mm, yy, span(which)].astype(F32).reshape(count, LANES)
            xf[t, pl.ds(pl.multiple_of(start, 8), count), :] = values

        widen(held, y, "all")
        for n in ARRIVALS:
            dz, dy, which, _ = MESSAGES[n]
            near_arrival(g, t, n).wait_recv()
            widen((held - dz + NEAR) % NEAR, 1 - y if dy else y, which)
        for k in range(chunks):
            out[t, :, k * LANES:(k + 1) * LANES] = xf[t, pl.ds(k, rows, stride=chunks), :].astype(BF16)

    def gather_sent(g, t):
        for j in range(nq):
            far_copy(g, t, j).wait_send()
        for n in range(len(MESSAGES)):
            near_copy(g, t, n).wait_send()

    def sum_copy(g, t, i):
        j = peer(i)
        return remote(
            f_out.at[g, t, j], f_in.at[g, t, i], f_send.at[0, g, t, i], f_recv.at[0, g, t, i], feature_devices[i - 1]
        )

    def sum_start(g, t, values):
        for i in range(1, nf):
            j = peer(i)
            start = pl.multiple_of(j // 2 * fb, 8)
            f_out[g, t, j] = values[t, j % 2, pl.ds(start, fb), :].astype(BF16)
            sum_copy(g, t, i).start()

    def sum_end(g, t, values):
        acc = values[t, side, pl.ds(pl.multiple_of(feat // 2 * fb, 8), fb), :]
        for i in range(1, nf):
            sum_copy(g, t, i).wait_recv()
            acc = acc + f_in[g, t, i].astype(F32)
        return acc

    def share_copy(t, i, mine):
        slot = codes.at[t, feat if mine else giver(i)]
        return remote(slot, slot, f_send.at[1, 0, t, i], f_recv.at[1, 0, t, i], feature_devices[i - 1])

    def share_start(t):
        for i in range(1, nf):
            share_copy(t, i, True).start()

    def share_end(t):
        for i in range(1, nf):
            share_copy(t, i, False).wait_recv()

    def give_copy(t, i):
        target = {"feature": peer(i), "latent": (z * 2 + y) * 2 + side}
        return remote(
            pre_own.at[t], pre_all.at[t, c, feat // 2], g_send.at[t, i], g_recv.at[t, c, feat // 2], target
        )

    def give_start(t):
        for i in range(1, nf):
            give_copy(t, i).start()

        @pl.when(side != c)
        def _():
            give_copy(t, 0).start()

        @pl.when(side == c)
        def _():
            pre_all[t, c, feat // 2] = pre_own[t]

    def give_end(t):
        for k in range(nf // 2):
            for cc in range(2):
                slot = pre_all.at[t, cc, k]
                arrival = remote(slot, slot, g_send.at[t, 0], g_recv.at[t, cc, k], other_core)

                @pl.when(jnp.logical_not((cc == c) & (2 * k + c == feat)))
                def _():
                    arrival.wait_recv()

    def give_sent(t):
        for i in range(1, nf):
            give_copy(t, i).wait_send()

        @pl.when(side != c)
        def _():
            give_copy(t, 0).wait_send()

    def sum_sent(g, t):
        for i in range(1, nf):
            sum_copy(g, t, i).wait_send()

    def local(t, mm, yy):
        start = (mm * 2 + yy) * group
        return blocks(xf[t, pl.ds(pl.multiple_of(start, 8), group), :])

    def blocks(value):
        return value.reshape(nq, rb, LANES)

    def rn_copy(t, n):
        dz, dy, which, slot = MESSAGES[n]
        mm = (held + dz + NEAR) % NEAR
        yy = 1 - y if dy else y
        return remote(
            near_out.at[t, mm, yy, span(which)], near_in.at[t, slot, span(which)],
            rn_s.at[t, n], rn_r.at[t, n], near_devices[n],
        )

    def reduce_near(t):
        for n, (dz, dy, which, _) in enumerate(MESSAGES):
            if which != "high":
                mm = (held + dz + NEAR) % NEAR
                yy = 1 - y if dy else y
                near_out[t, mm, yy] = local(t, mm, yy).astype(BF16)
            rn_copy(t, n).start()

    def rf_copy(t, j):
        return remote(far_out.at[t, j], far_in.at[t, j], rf_s.at[t, j], rf_r.at[t, j], far_devices[nq - 1 - j])

    def reduce_far(t):
        total[t] = local(t, held, y)
        for n in ARRIVALS:
            _, _, which, slot = MESSAGES[n]
            rn_copy(t, n).wait_recv()
            total[t, span(which)] = total[t, span(which)] + near_in[t, slot, span(which)].astype(F32)
        for j in far_order:
            far_out[t, j] = total[t, far_blocks[j]].astype(BF16)
            rf_copy(t, j).start()

    def reduce_end(t):
        acc = jnp.zeros((rb, LANES), F32)
        for j in reversed(far_order):
            rf_copy(t, j).wait_recv()
            acc = acc + far_in[t, j].astype(F32)
        own[1, t] = (acc - goal[t]).astype(BF16)
        total_rows[t] = acc

    def write_recon(t):
        for k in range(chunks):
            wide_rows[:, t, k * LANES:(k + 1) * LANES] = total_rows[t, pl.ds(k, own_rows, stride=chunks), :]

    def reduce_sent(t):
        for n in range(len(MESSAGES)):
            rn_copy(t, n).wait_send()
        for j in range(nq):
            rf_copy(t, j).wait_send()

    both = (0, 1)
    for t in both:
        gather_far(0, t)
    for copy in swaps:
        copy.start()
    for t in both:
        gather_near(0, t)
    load_enc.wait()
    for copy in swapped[:2]:
        copy.wait_recv()
    for t in both:
        gather_end(0, t, a_own)
        for cc in range(2):
            part[t, cc] = jnp.dot(a_own[t], enc[cc, t], preferred_element_type=F32)
        sum_start(0, t, part)
    store_act = [pltpu.make_async_copy(a_own.at[t], a_hbm.at[t, c], load_sem.at[2 + t]) for t in both]
    for t in both:
        store_act[t].start()
        act_copy(t).start()
        value = sum_end(0, t, part) + biases[side, t:t + 1, :]
        codes[t, feat] = (mask[t] * value).astype(BF16)
        share_start(t)
    load_dec.wait()
    swapped[2].wait_recv()

    def whole(t, cc):
        mine = [codes[t, 2 * k + cc].astype(F32) for k in range(nf // 2)]
        return jnp.concatenate(mine, axis=0)

    wide = 2 * LANES
    for t in both:
        share_end(t)
        terms = []
        for cc in range(2):
            if t == 0:
                terms.append((whole(0, cc).astype(BF16), cc, 0))
            else:
                lanes = slice(cc * latents, (cc + 1) * latents)
                terms.append(((whole(0, cc) * gate[:, lanes]).astype(BF16), cc, 1))
                terms.append((whole(1, cc).astype(BF16), cc, 2))
        for n in range(depth // wide):
            cols = slice(n * wide, (n + 1) * wide)
            value = sum(jnp.dot(code, dec[cc, p, :, cols], preferred_element_type=F32) for code, cc, p in terms)
            for k in range(2):
                xf[t, pl.ds(2 * n + k, rows, stride=chunks), :] = value[:, k * LANES:(k + 1) * LANES]
        reduce_near(t)
    for copy in swaps:
        copy.wait_send()
    for t in both:
        gather_sent(0, t)
        sum_sent(0, t)
        for i in range(1, nf):
            share_copy(t, i, True).wait_send()
    for t in both:
        reduce_far(t)
    for t in both:
        reduce_end(t)
        gather_far(1, t)
    for t in both:
        gather_near(1, t)
    for t in both:
        reduce_sent(t)
        write_recon(t)
    recon[...] = wide_rows[...].astype(BF16)
    store_recon = pltpu.make_async_copy(recon, recon_hbm, small_sem.at[0])
    store_recon.start()

    def gradient(t, cc, p):
        return lax.dot_general(err_own[t], dec[cc, p], across, preferred_element_type=F32)

    gather_end(1, 0, err_own)
    for cc in range(2):
        grad[0, cc] = gradient(0, cc, 0)
    gather_end(1, 1, err_own)
    for cc in range(2):
        grad[1, cc] = gradient(1, cc, 2)
    sum_start(1, 1, grad)
    for cc in range(2):
        grad[0, cc] = grad[0, cc] + gate[:, cc * latents:(cc + 1) * latents] * gradient(1, cc, 1)
    sum_start(1, 0, grad)
    for t in (1, 0):
        pre_own[t] = (mask[t] * sum_end(1, t, grad) * scale).astype(BF16)
        give_start(t)
    for t in both:
        gather_sent(1, t)
        sum_sent(1, t)
        store_act[t].wait()
        act_copy(t).wait_send()
        arrived = a_hbm.at[t, 1 - c]
        remote(arrived, arrived, swap_s.at[3 + t], swap_r.at[3 + t], other_core).wait_recv()
    store_pre = [pltpu.make_async_copy(pre_out.at[t], pre_hbm.at[t], small_sem.at[1 + t]) for t in both]
    for t in (1, 0):
        give_end(t)
        for cc in range(2):
            whole_rows = jnp.concatenate([pre_all[t, cc, k].astype(F32) for k in range(nf // 2)], axis=0)
            pre_out[t, cc] = whole_rows.astype(BF16)
        store_pre[t].start()
    store_recon.wait()
    for t in both:
        give_sent(t)
        store_pre[t].wait()


def body(nz, nf, activations, targets, enc_weight, enc_bias, dec_weight, top_blocks, pair_mask):
    own_rows, layers, depth = activations.shape
    all_rows = top_blocks.shape[0]
    rows = all_rows // 2
    latents = enc_weight.shape[2]
    chunks = depth // LANES
    rb = own_rows * chunks
    fb = all_rows // nf
    nq = nz // NEAR
    hbm = pl.BlockSpec(memory_space=pltpu.HBM)
    dma = pltpu.SemaphoreType.DMA
    bf, f32 = (lambda *s: pltpu.VMEM(s, BF16)), (lambda *s: pltpu.VMEM(s, F32))
    count = len(MESSAGES)
    recon, a_all, pre_grad = pl.pallas_call(
        functools.partial(kernel, nz, nf, 1.0 / math.sqrt(all_rows)),
        out_shape=(
            jax.ShapeDtypeStruct(activations.shape, BF16),
            jax.ShapeDtypeStruct((layers, 2, rows, depth), BF16),
            jax.ShapeDtypeStruct((layers, 2, rows, latents), BF16),
        ),
        in_specs=[hbm] * 7,
        out_specs=(hbm, hbm, hbm),
        scratch_shapes=[
            bf(*activations.shape),
            bf(*targets.shape),
            f32(*enc_bias.shape),
            pltpu.VMEM((layers, top_blocks.shape[2], all_rows), jnp.int32),
            pltpu.VMEM(pair_mask.shape, jnp.int32),
            bf(*activations.shape),
            bf(layers, 2, rows, latents),
            bf(layers, rows, depth),
            bf(2, *enc_weight.shape),
            bf(2, *dec_weight.shape),
            f32(2, *enc_bias.shape),
            bf(2, layers, rb, LANES),
            f32(layers, rb, LANES),
            f32(own_rows, layers, depth),
            f32(layers, fb, latents),
            f32(1, 2 * latents),
            bf(2, layers, NEAR, 2, nq, rb, LANES),
            f32(layers, rows * chunks, LANES),
            bf(layers, rows, depth),
            f32(layers, 2, rows, latents),
            f32(layers, 2, rows, latents),
            bf(2, layers, nf, fb, latents),
            bf(2, layers, nf, fb, latents),
            bf(layers, nf, fb, latents),
            bf(layers, fb, latents),
            bf(layers, 2, nf // 2, fb, latents),
            bf(layers, NEAR, 2, nq, rb, LANES),
            bf(layers, SLOTS, nq, rb, LANES),
            f32(layers, nq, rb, LANES),
            f32(layers, rb, LANES),
            bf(layers, nq, rb, LANES),
            bf(layers, nq, rb, LANES),
            dma((4,)),
            dma((5,)),
            dma((5,)),
            dma((5,)),
            dma((2, layers, nq)),
            dma((2, layers, nq)),
            dma((2, layers, count)),
            dma((2, layers, count)),
            dma((2, 2, layers, nf)),
            dma((2, 2, layers, nf)),
            dma((layers, nf)),
            dma((layers, 2, nf // 2)),
            dma((layers, count)),
            dma((layers, count)),
            dma((layers, nq)),
            dma((layers, nq)),
        ],
        compiler_params=pltpu.CompilerParams(
            collective_id=0, has_side_effects=True, vmem_limit_bytes=63 * 2**20
        ),
    )(
        activations, targets, enc_weight, enc_bias, dec_weight, top_blocks.transpose(1, 2, 0), pair_mask,
    )
    enc_grad = jnp.einsum(
        "lrd,lrf->ldf",
        a_all.reshape(layers, all_rows, depth),
        pre_grad.reshape(layers, all_rows, latents),
        preferred_element_type=F32,
    )
    return recon, enc_grad


def solution(mesh):
    in_specs = (
        P("latent", None, "feature"),
        P("latent", None, "feature"),
        P(None, "feature", "latent"),
        P(None, "latent"),
        P(None, "latent", "feature"),
        P(),
        P(),
    )
    out_specs = (P("latent", None, "feature"), P(None, "feature", "latent"))
    step = functools.partial(body, mesh.shape["latent"] // 4, mesh.shape["feature"])
    return jax.shard_map(step, mesh=mesh, in_specs=in_specs, out_specs=out_specs, check_vma=False)
```

```python
import functools
import math

import jax
import jax.numpy as jnp
from jax import lax
from jax.experimental import pallas as pl
from jax.experimental.pallas import tpu as pltpu
from jax.sharding import PartitionSpec as P

BLOCK = 128
LANES = 128
F32 = jnp.float32
BF16 = jnp.bfloat16
MESH = pl.DeviceIdType.MESH
NEAR = 4
MESSAGES = (
    (2, 1, "low", 5), (-2, 1, "high", 5), (1, 1, "all", 1), (-1, 1, "all", 3),
    (2, 0, "low", 4), (-2, 0, "high", 4), (0, 1, "all", 6), (1, 0, "all", 0), (-1, 0, "all", 2),
)
ARRIVALS = (7, 8, 4, 5, 6, 2, 3, 0, 1)
SLOTS = 7


def kernel(
    nz, nf, scale,
    act_hbm, tgt_hbm, enc_hbm, bias_hbm, dec_hbm, top_hbm, pairs_hbm,
    recon_hbm, a_hbm, pre_hbm,
    act, tgt, bias, top, pairs, recon, pre_out, a_own, enc, dec, biases, own, goal, wide_rows, mask, gate, x, xf, err_own, part, grad,
    f_out, f_in, codes, pre_own, pre_all,
    near_out, near_in, total, total_rows, far_out, far_in,
    load_sem, small_sem, swap_s, swap_r, far_s, far_r, near_s, near_r,
    f_send, f_recv, g_send, g_recv, rn_s, rn_r, rf_s, rf_r,
):
    feat = lax.axis_index("feature")
    lat = lax.axis_index("latent")
    c = lat % 2
    y = (lat // 2) % 2
    z = lat // 4
    nq = nz // NEAR
    held = (z + 2) % NEAR
    offsets = [2 - nz // 2 + NEAR * j for j in range(nq)]
    own_rows = act.shape[0]
    inputs = ((act_hbm, act), (tgt_hbm, tgt), (bias_hbm, bias), (top_hbm, top), (pairs_hbm, pairs))
    loads = [pltpu.make_async_copy(a, b, small_sem.at[i]) for i, (a, b) in enumerate(inputs)]
    rb = own.shape[2]
    rows, depth = a_own.shape[1:]
    chunks = depth // LANES
    latents = enc.shape[3]
    fb = 2 * rows // nf
    side = feat % 2
    group = nq * rb

    def at(zz, yy, cc):
        return {"latent": (((zz + nz) % nz) * 2 + yy) * 2 + cc}

    other_core = at(z, y, 1 - c)
    near_devices = [at(z + dz, 1 - y if dy else y, c) for dz, dy, _, _ in MESSAGES]
    far_devices = [at(z + o, y, c) for o in offsets]
    far_order = sorted(range(nq), key=lambda j: -abs(offsets[j]))
    far_blocks = [((z - o + nz) % nz) // NEAR for o in offsets]
    parts = {"all": slice(0, nq), "low": slice(0, nq // 2), "high": slice(nq // 2, nq)}

    def span(which):
        s = parts[which]
        return pl.ds(s.start, s.stop - s.start)

    relations = [(0, 0)] + [(a, b) for a, b in ((1, 2), (0, 2), (1, 1), (1, 3), (0, 1), (0, 3), (1, 0))]

    def peer(i):
        a, b = relations[i]
        return (feat // 4 + a) % 2 * 4 + (feat % 4 + b) % 4

    def giver(i):
        a, b = relations[i]
        return (feat // 4 + a) % 2 * 4 + (feat % 4 + 4 - b) % 4

    feature_devices = [{"feature": peer(i)} for i in range(1, nf)]
    cross_devices = [{"feature": peer(i), "latent": (z * 2 + y) * 2 + 1 - c} for i in range(1, nf)]
    everyone = [far_devices[j] for j in far_order] + cross_devices + feature_devices + near_devices + [other_core]
    barrier = pltpu.get_barrier_semaphore()
    for device in everyone:
        pl.semaphore_signal(barrier, inc=1, device_id=device, device_id_type=MESH)
    for copy in loads:
        copy.start()
    load_enc = pltpu.make_async_copy(enc_hbm, enc.at[c], load_sem.at[0])
    load_dec = pltpu.make_async_copy(dec_hbm, dec.at[c], load_sem.at[1])
    load_enc.start()
    load_dec.start()

    for copy in loads:
        copy.wait()

    def split(ref, t, put):
        values = ref[...].astype(F32)
        for k in range(chunks):
            put[t, pl.ds(k, own_rows, stride=chunks), :] = values[:, t, k * LANES:(k + 1) * LANES]

    for t in range(2):
        split(act, t, total_rows)
        own[0, t] = total_rows[t].astype(BF16)
        split(tgt, t, goal)
    local_blocks = latents // BLOCK
    place = feat // 2 * fb + lax.broadcasted_iota(jnp.int32, (fb, rows * 2), 0)
    first = ((z * 2 + y) * 2 + side) * local_blocks
    index = lax.div(place, own_rows)
    device = lax.rem(index, nq) * (4 * NEAR) + lax.div(index, nq) * 2 + c
    source = device * own_rows + lax.rem(place, own_rows)
    picked = source == lax.broadcasted_iota(jnp.int32, (fb, rows * 2), 1)
    picked = jnp.where(picked, 1.0, 0.0).astype(BF16)
    across = (((1,), (1,)), ((), ()))
    for t in range(2):
        hits = []
        for b in range(local_blocks):
            same = jnp.where(top[t] == first + b, 1.0, 0.0)
            hits.append(jnp.broadcast_to(jnp.sum(same, axis=0, keepdims=True), (BLOCK, rows * 2)))
        hits = jnp.concatenate(hits, axis=0).astype(BF16)
        mask[t] = lax.dot_general(picked, hits, across, preferred_element_type=F32)
    numbers = pairs[0].astype(F32)[1:2]
    lanes = lax.broadcasted_iota(jnp.int32, numbers.shape, 1)
    for b in range(2 * local_blocks):
        chosen = lanes == (z * 2 + y) * 2 * local_blocks + b
        value = jnp.sum(jnp.where(chosen, numbers, 0.0), axis=1, keepdims=True)
        gate[:, b * BLOCK:(b + 1) * BLOCK] = jnp.broadcast_to(value, (1, BLOCK))
    biases[c] = bias[...]
    pl.semaphore_wait(barrier, len(everyone))

    def remote(src, dst, send, recv, device):
        return pltpu.make_async_remote_copy(
            src_ref=src, dst_ref=dst, send_sem=send, recv_sem=recv, device_id=device, device_id_type=MESH
        )

    swaps = [
        remote(ref, out, swap_s.at[i], swap_r.at[i], other_core)
        for i, (ref, out) in enumerate(((bias, biases.at[c]), (enc_hbm, enc.at[c]), (dec_hbm, dec.at[c])))
    ]
    swapped = [
        remote(out, out, swap_s.at[i], swap_r.at[i], other_core)
        for i, out in enumerate((biases.at[1 - c], enc.at[1 - c], dec.at[1 - c]))
    ]

    def act_copy(t):
        return remote(a_own.at[t], a_hbm.at[t, c], swap_s.at[3 + t], swap_r.at[3 + t], other_core)

    def far_copy(g, t, j):
        ref = x.at[g, t, z % NEAR, y, z // NEAR]
        return remote(own.at[g, t], ref, far_s.at[g, t, j], far_r.at[g, t, j], far_devices[j])

    def far_arrival(g, t, j):
        ref = x.at[g, t, held, y, far_blocks[j]]
        return remote(ref, ref, far_s.at[g, t, j], far_r.at[g, t, j], far_devices[j])

    def near_copy(g, t, n):
        ref = x.at[g, t, held, y, span(MESSAGES[n][2])]
        return remote(ref, ref, near_s.at[g, t, n], near_r.at[g, t, n], near_devices[n])

    def near_arrival(g, t, n):
        dz, dy, which, _ = MESSAGES[n]
        ref = x.at[g, t, (held - dz + NEAR) % NEAR, 1 - y if dy else y, span(which)]
        return remote(ref, ref, near_s.at[g, t, n], near_r.at[g, t, n], near_devices[n])

    def gather_far(g, t):
        for j in far_order:
            far_copy(g, t, j).start()

    def gather_near(g, t):
        for j in range(nq):
            far_arrival(g, t, j).wait_recv()
        for n in range(len(MESSAGES)):
            near_copy(g, t, n).start()

    def gather_end(g, t, out):
        def widen(mm, yy, which):
            piece = parts[which]
            count = (piece.stop - piece.start) * rb
            start = ((mm * 2 + yy) * nq + piece.start) * rb
            values = x[g, t, mm, yy, span(which)].astype(F32).reshape(count, LANES)
            xf[t, pl.ds(pl.multiple_of(start, 8), count), :] = values

        widen(held, y, "all")
        for n in ARRIVALS:
            dz, dy, which, _ = MESSAGES[n]
            near_arrival(g, t, n).wait_recv()
            widen((held - dz + NEAR) % NEAR, 1 - y if dy else y, which)
        for k in range(chunks):
            out[t, :, k * LANES:(k + 1) * LANES] = xf[t, pl.ds(k, rows, stride=chunks), :].astype(BF16)

    def gather_sent(g, t):
        for j in range(nq):
            far_copy(g, t, j).wait_send()
        for n in range(len(MESSAGES)):
            near_copy(g, t, n).wait_send()

    def sum_copy(g, t, i):
        j = peer(i)
        return remote(
            f_out.at[g, t, j], f_in.at[g, t, i], f_send.at[0, g, t, i], f_recv.at[0, g, t, i], feature_devices[i - 1]
        )

    def sum_start(g, t, values):
        for i in range(1, nf):
            j = peer(i)
            start = pl.multiple_of(j // 2 * fb, 8)
            f_out[g, t, j] = values[t, j % 2, pl.ds(start, fb), :].astype(BF16)
            sum_copy(g, t, i).start()

    def sum_end(g, t, values):
        acc = values[t, side, pl.ds(pl.multiple_of(feat // 2 * fb, 8), fb), :]
        for i in range(1, nf):
            sum_copy(g, t, i).wait_recv()
            acc = acc + f_in[g, t, i].astype(F32)
        return acc

    def share_copy(t, i, mine):
        slot = codes.at[t, feat if mine else giver(i)]
        return remote(slot, slot, f_send.at[1, 0, t, i], f_recv.at[1, 0, t, i], feature_devices[i - 1])

    def share_start(t):
        for i in range(1, nf):
            share_copy(t, i, True).start()

    def share_end(t):
        for i in range(1, nf):
            share_copy(t, i, False).wait_recv()

    def give_copy(t, i):
        target = {"feature": peer(i), "latent": (z * 2 + y) * 2 + side}
        return remote(
            pre_own.at[t], pre_all.at[t, c, feat // 2], g_send.at[t, i], g_recv.at[t, c, feat // 2], target
        )

    def give_start(t):
        for i in range(1, nf):
            give_copy(t, i).start()

        @pl.when(side != c)
        def _():
            give_copy(t, 0).start()

        @pl.when(side == c)
        def _():
            pre_all[t, c, feat // 2] = pre_own[t]

    def give_end(t):
        for k in range(nf // 2):
            for cc in range(2):
                slot = pre_all.at[t, cc, k]
                arrival = remote(slot, slot, g_send.at[t, 0], g_recv.at[t, cc, k], other_core)

                @pl.when(jnp.logical_not((cc == c) & (2 * k + c == feat)))
                def _():
                    arrival.wait_recv()

    def give_sent(t):
        for i in range(1, nf):
            give_copy(t, i).wait_send()

        @pl.when(side != c)
        def _():
            give_copy(t, 0).wait_send()

    def sum_sent(g, t):
        for i in range(1, nf):
            sum_copy(g, t, i).wait_send()

    def local(t, mm, yy):
        start = (mm * 2 + yy) * group
        return blocks(xf[t, pl.ds(pl.multiple_of(start, 8), group), :])

    def blocks(value):
        return value.reshape(nq, rb, LANES)

    def rn_copy(t, n):
        dz, dy, which, slot = MESSAGES[n]
        mm = (held + dz + NEAR) % NEAR
        yy = 1 - y if dy else y
        return remote(
            near_out.at[t, mm, yy, span(which)], near_in.at[t, slot, span(which)],
            rn_s.at[t, n], rn_r.at[t, n], near_devices[n],
        )

    def reduce_near(t):
        for n, (dz, dy, which, _) in enumerate(MESSAGES):
            if which != "high":
                mm = (held + dz + NEAR) % NEAR
                yy = 1 - y if dy else y
                near_out[t, mm, yy] = local(t, mm, yy).astype(BF16)
            rn_copy(t, n).start()

    def rf_copy(t, j):
        return remote(far_out.at[t, j], far_in.at[t, j], rf_s.at[t, j], rf_r.at[t, j], far_devices[nq - 1 - j])

    def reduce_far(t):
        total[t] = local(t, held, y)
        for n in ARRIVALS:
            _, _, which, slot = MESSAGES[n]
            rn_copy(t, n).wait_recv()
            total[t, span(which)] = total[t, span(which)] + near_in[t, slot, span(which)].astype(F32)
        for j in far_order:
            far_out[t, j] = total[t, far_blocks[j]].astype(BF16)
            rf_copy(t, j).start()

    def reduce_end(t):
        acc = jnp.zeros((rb, LANES), F32)
        for j in reversed(far_order):
            rf_copy(t, j).wait_recv()
            acc = acc + far_in[t, j].astype(F32)
        own[1, t] = (acc - goal[t]).astype(BF16)
        total_rows[t] = acc

    def write_recon(t):
        for k in range(chunks):
            wide_rows[:, t, k * LANES:(k + 1) * LANES] = total_rows[t, pl.ds(k, own_rows, stride=chunks), :]

    def reduce_sent(t):
        for n in range(len(MESSAGES)):
            rn_copy(t, n).wait_send()
        for j in range(nq):
            rf_copy(t, j).wait_send()

    both = (0, 1)
    for t in both:
        gather_far(0, t)
    for t in both:
        gather_near(0, t)
    for copy in swaps:
        copy.start()
    load_enc.wait()
    for copy in swapped[:2]:
        copy.wait_recv()
    for t in both:
        gather_end(0, t, a_own)
        for cc in range(2):
            part[t, cc] = jnp.dot(a_own[t], enc[cc, t], preferred_element_type=F32)
        sum_start(0, t, part)
    store_act = [pltpu.make_async_copy(a_own.at[t], a_hbm.at[t, c], load_sem.at[2 + t]) for t in both]
    for t in both:
        store_act[t].start()
        act_copy(t).start()
        value = sum_end(0, t, part) + biases[side, t:t + 1, :]
        codes[t, feat] = (mask[t] * value).astype(BF16)
        share_start(t)
    load_dec.wait()
    swapped[2].wait_recv()

    def whole(t, cc):
        mine = [codes[t, 2 * k + cc].astype(F32) for k in range(nf // 2)]
        return jnp.concatenate(mine, axis=0)

    wide = 2 * LANES
    for t in both:
        share_end(t)
        terms = []
        for cc in range(2):
            if t == 0:
                terms.append((whole(0, cc).astype(BF16), cc, 0))
            else:
                lanes = slice(cc * latents, (cc + 1) * latents)
                terms.append(((whole(0, cc) * gate[:, lanes]).astype(BF16), cc, 1))
                terms.append((whole(1, cc).astype(BF16), cc, 2))
        for n in range(depth // wide):
            cols = slice(n * wide, (n + 1) * wide)
            value = sum(jnp.dot(code, dec[cc, p, :, cols], preferred_element_type=F32) for code, cc, p in terms)
            for k in range(2):
                xf[t, pl.ds(2 * n + k, rows, stride=chunks), :] = value[:, k * LANES:(k + 1) * LANES]
        reduce_near(t)
    for copy in swaps:
        copy.wait_send()
    for t in both:
        gather_sent(0, t)
        sum_sent(0, t)
        for i in range(1, nf):
            share_copy(t, i, True).wait_send()
    for t in both:
        reduce_far(t)
    for t in both:
        reduce_end(t)
        gather_far(1, t)
    for t in both:
        gather_near(1, t)
    for t in both:
        reduce_sent(t)
        write_recon(t)
    recon[...] = wide_rows[...].astype(BF16)
    store_recon = pltpu.make_async_copy(recon, recon_hbm, small_sem.at[0])
    store_recon.start()

    def gradient(t, cc, p):
        return lax.dot_general(err_own[t], dec[cc, p], across, preferred_element_type=F32)

    gather_end(1, 0, err_own)
    for cc in range(2):
        grad[0, cc] = gradient(0, cc, 0)
    gather_end(1, 1, err_own)
    for cc in range(2):
        grad[1, cc] = gradient(1, cc, 2)
    sum_start(1, 1, grad)
    for cc in range(2):
        grad[0, cc] = grad[0, cc] + gate[:, cc * latents:(cc + 1) * latents] * gradient(1, cc, 1)
    sum_start(1, 0, grad)
    for t in (1, 0):
        pre_own[t] = (mask[t] * sum_end(1, t, grad) * scale).astype(BF16)
        give_start(t)
    for t in both:
        gather_sent(1, t)
        sum_sent(1, t)
        store_act[t].wait()
        act_copy(t).wait_send()
        arrived = a_hbm.at[t, 1 - c]
        remote(arrived, arrived, swap_s.at[3 + t], swap_r.at[3 + t], other_core).wait_recv()
    store_pre = [pltpu.make_async_copy(pre_out.at[t], pre_hbm.at[t], small_sem.at[1 + t]) for t in both]
    for t in (1, 0):
        give_end(t)
        for cc in range(2):
            whole_rows = jnp.concatenate([pre_all[t, cc, k].astype(F32) for k in range(nf // 2)], axis=0)
            pre_out[t, cc] = whole_rows.astype(BF16)
        store_pre[t].start()
    store_recon.wait()
    for t in both:
        give_sent(t)
        store_pre[t].wait()


def body(nz, nf, activations, targets, enc_weight, enc_bias, dec_weight, top_blocks, pair_mask):
    own_rows, layers, depth = activations.shape
    all_rows = top_blocks.shape[0]
    rows = all_rows // 2
    latents = enc_weight.shape[2]
    chunks = depth // LANES
    rb = own_rows * chunks
    fb = all_rows // nf
    nq = nz // NEAR
    hbm = pl.BlockSpec(memory_space=pltpu.HBM)
    dma = pltpu.SemaphoreType.DMA
    bf, f32 = (lambda *s: pltpu.VMEM(s, BF16)), (lambda *s: pltpu.VMEM(s, F32))
    count = len(MESSAGES)
    recon, a_all, pre_grad = pl.pallas_call(
        functools.partial(kernel, nz, nf, 1.0 / math.sqrt(all_rows)),
        out_shape=(
            jax.ShapeDtypeStruct(activations.shape, BF16),
            jax.ShapeDtypeStruct((layers, 2, rows, depth), BF16),
            jax.ShapeDtypeStruct((layers, 2, rows, latents), BF16),
        ),
        in_specs=[hbm] * 7,
        out_specs=(hbm, hbm, hbm),
        scratch_shapes=[
            bf(*activations.shape),
            bf(*targets.shape),
            f32(*enc_bias.shape),
            pltpu.VMEM((layers, top_blocks.shape[2], all_rows), jnp.int32),
            pltpu.VMEM(pair_mask.shape, jnp.int32),
            bf(*activations.shape),
            bf(layers, 2, rows, latents),
            bf(layers, rows, depth),
            bf(2, *enc_weight.shape),
            bf(2, *dec_weight.shape),
            f32(2, *enc_bias.shape),
            bf(2, layers, rb, LANES),
            f32(layers, rb, LANES),
            f32(own_rows, layers, depth),
            f32(layers, fb, latents),
            f32(1, 2 * latents),
            bf(2, layers, NEAR, 2, nq, rb, LANES),
            f32(layers, rows * chunks, LANES),
            bf(layers, rows, depth),
            f32(layers, 2, rows, latents),
            f32(layers, 2, rows, latents),
            bf(2, layers, nf, fb, latents),
            bf(2, layers, nf, fb, latents),
            bf(layers, nf, fb, latents),
            bf(layers, fb, latents),
            bf(layers, 2, nf // 2, fb, latents),
            bf(layers, NEAR, 2, nq, rb, LANES),
            bf(layers, SLOTS, nq, rb, LANES),
            f32(layers, nq, rb, LANES),
            f32(layers, rb, LANES),
            bf(layers, nq, rb, LANES),
            bf(layers, nq, rb, LANES),
            dma((4,)),
            dma((5,)),
            dma((5,)),
            dma((5,)),
            dma((2, layers, nq)),
            dma((2, layers, nq)),
            dma((2, layers, count)),
            dma((2, layers, count)),
            dma((2, 2, layers, nf)),
            dma((2, 2, layers, nf)),
            dma((layers, nf)),
            dma((layers, 2, nf // 2)),
            dma((layers, count)),
            dma((layers, count)),
            dma((layers, nq)),
            dma((layers, nq)),
        ],
        compiler_params=pltpu.CompilerParams(
            collective_id=0, has_side_effects=True, vmem_limit_bytes=63 * 2**20
        ),
    )(
        activations, targets, enc_weight, enc_bias, dec_weight, top_blocks.transpose(1, 2, 0), pair_mask,
    )
    enc_grad = jnp.einsum(
        "lrd,lrf->ldf",
        a_all.reshape(layers, all_rows, depth),
        pre_grad.reshape(layers, all_rows, latents),
        preferred_element_type=F32,
    )
    return recon, enc_grad


def solution(mesh):
    in_specs = (
        P("latent", None, "feature"),
        P("latent", None, "feature"),
        P(None, "feature", "latent"),
        P(None, "latent"),
        P(None, "latent", "feature"),
        P(),
        P(),
    )
    out_specs = (P("latent", None, "feature"), P(None, "feature", "latent"))
    step = functools.partial(body, mesh.shape["latent"] // 4, mesh.shape["feature"])
    return jax.shard_map(step, mesh=mesh, in_specs=in_specs, out_specs=out_specs, check_vma=False)
```

```python
import functools
import math

import jax
import jax.numpy as jnp
from jax import lax
from jax.experimental import pallas as pl
from jax.experimental.pallas import tpu as pltpu
from jax.sharding import PartitionSpec as P

BLOCK = 128
LANES = 128
F32 = jnp.float32
BF16 = jnp.bfloat16
MESH = pl.DeviceIdType.MESH
NEAR = 4
MESSAGES = (
    (2, 1, "low", 5), (-2, 1, "high", 5), (1, 1, "all", 1), (-1, 1, "all", 3),
    (2, 0, "low", 4), (-2, 0, "high", 4), (0, 1, "all", 6), (1, 0, "all", 0), (-1, 0, "all", 2),
)
ARRIVALS = (7, 8, 4, 5, 6, 2, 3, 0, 1)
SLOTS = 7


def kernel(
    nz, nf, scale,
    act_hbm, tgt_hbm, enc_hbm, bias_hbm, dec_hbm, top_hbm, pairs_hbm,
    recon_hbm, a_hbm, pre_hbm,
    act, tgt, bias, top, pairs, recon, pre_out, a_own, enc, dec, biases, own, goal, wide_rows, mask, gate, x, xf, err_own, part, grad,
    f_out, f_in, codes, pre_own, pre_all,
    near_out, near_in, total, total_rows, far_out, far_in,
    load_sem, small_sem, swap_s, swap_r, far_s, far_r, near_s, near_r,
    f_send, f_recv, g_send, g_recv, rn_s, rn_r, rf_s, rf_r,
):
    feat = lax.axis_index("feature")
    lat = lax.axis_index("latent")
    c = lat % 2
    y = (lat // 2) % 2
    z = lat // 4
    nq = nz // NEAR
    held = (z + 2) % NEAR
    offsets = [2 - nz // 2 + NEAR * j for j in range(nq)]
    own_rows = act.shape[0]
    inputs = ((act_hbm, act), (tgt_hbm, tgt), (bias_hbm, bias), (top_hbm, top), (pairs_hbm, pairs))
    loads = [pltpu.make_async_copy(a, b, small_sem.at[i]) for i, (a, b) in enumerate(inputs)]
    rb = own.shape[2]
    rows, depth = a_own.shape[1:]
    chunks = depth // LANES
    latents = enc.shape[3]
    fb = 2 * rows // nf
    side = feat % 2
    group = nq * rb

    def at(zz, yy, cc):
        return {"latent": (((zz + nz) % nz) * 2 + yy) * 2 + cc}

    other_core = at(z, y, 1 - c)
    near_devices = [at(z + dz, 1 - y if dy else y, c) for dz, dy, _, _ in MESSAGES]
    far_devices = [at(z + o, y, c) for o in offsets]
    far_order = sorted(range(nq), key=lambda j: -abs(offsets[j]))
    far_blocks = [((z - o + nz) % nz) // NEAR for o in offsets]
    parts = {"all": slice(0, nq), "low": slice(0, nq // 2), "high": slice(nq // 2, nq)}

    def span(which):
        s = parts[which]
        return pl.ds(s.start, s.stop - s.start)

    relations = [(0, 0)] + [(a, b) for a, b in ((1, 2), (0, 2), (1, 1), (1, 3), (0, 1), (0, 3), (1, 0))]

    def peer(i):
        a, b = relations[i]
        return (feat // 4 + a) % 2 * 4 + (feat % 4 + b) % 4

    def giver(i):
        a, b = relations[i]
        return (feat // 4 + a) % 2 * 4 + (feat % 4 + 4 - b) % 4

    feature_devices = [{"feature": peer(i)} for i in range(1, nf)]
    cross_devices = [{"feature": peer(i), "latent": (z * 2 + y) * 2 + 1 - c} for i in range(1, nf)]
    everyone = [far_devices[j] for j in far_order] + cross_devices + feature_devices + near_devices + [other_core]
    barrier = pltpu.get_barrier_semaphore()
    for device in everyone:
        pl.semaphore_signal(barrier, inc=1, device_id=device, device_id_type=MESH)
    for copy in loads:
        copy.start()
    load_enc = pltpu.make_async_copy(enc_hbm, enc.at[c], load_sem.at[0])
    load_dec = pltpu.make_async_copy(dec_hbm, dec.at[c], load_sem.at[1])
    load_enc.start()
    load_dec.start()

    for copy in loads:
        copy.wait()

    def split(ref, t, put):
        values = ref[...].astype(F32)
        for k in range(chunks):
            put[t, pl.ds(k, own_rows, stride=chunks), :] = values[:, t, k * LANES:(k + 1) * LANES]

    for t in range(2):
        split(act, t, total_rows)
        own[0, t] = total_rows[t].astype(BF16)
        split(tgt, t, goal)
    local_blocks = latents // BLOCK
    place = feat // 2 * fb + lax.broadcasted_iota(jnp.int32, (fb, rows * 2), 0)
    first = ((z * 2 + y) * 2 + side) * local_blocks
    index = lax.div(place, own_rows)
    device = lax.rem(index, nq) * (4 * NEAR) + lax.div(index, nq) * 2 + c
    source = device * own_rows + lax.rem(place, own_rows)
    picked = source == lax.broadcasted_iota(jnp.int32, (fb, rows * 2), 1)
    picked = jnp.where(picked, 1.0, 0.0).astype(BF16)
    across = (((1,), (1,)), ((), ()))
    for t in range(2):
        hits = []
        for b in range(local_blocks):
            same = jnp.where(top[t] == first + b, 1.0, 0.0)
            hits.append(jnp.broadcast_to(jnp.sum(same, axis=0, keepdims=True), (BLOCK, rows * 2)))
        hits = jnp.concatenate(hits, axis=0).astype(BF16)
        mask[t] = lax.dot_general(picked, hits, across, preferred_element_type=F32)
    numbers = pairs[0].astype(F32)[1:2]
    lanes = lax.broadcasted_iota(jnp.int32, numbers.shape, 1)
    for b in range(2 * local_blocks):
        chosen = lanes == (z * 2 + y) * 2 * local_blocks + b
        value = jnp.sum(jnp.where(chosen, numbers, 0.0), axis=1, keepdims=True)
        gate[:, b * BLOCK:(b + 1) * BLOCK] = jnp.broadcast_to(value, (1, BLOCK))
    biases[c] = bias[...]
    pl.semaphore_wait(barrier, len(everyone))

    def remote(src, dst, send, recv, device):
        return pltpu.make_async_remote_copy(
            src_ref=src, dst_ref=dst, send_sem=send, recv_sem=recv, device_id=device, device_id_type=MESH
        )

    swaps = [
        remote(ref, out, swap_s.at[i], swap_r.at[i], other_core)
        for i, (ref, out) in enumerate(((bias, biases.at[c]), (enc_hbm, enc.at[c]), (dec_hbm, dec.at[c])))
    ]
    swapped = [
        remote(out, out, swap_s.at[i], swap_r.at[i], other_core)
        for i, out in enumerate((biases.at[1 - c], enc.at[1 - c], dec.at[1 - c]))
    ]

    def act_copy(t):
        return remote(a_own.at[t], a_hbm.at[t, c], swap_s.at[3 + t], swap_r.at[3 + t], other_core)

    def far_copy(g, t, j):
        ref = x.at[g, t, z % NEAR, y, z // NEAR]
        return remote(own.at[g, t], ref, far_s.at[g, t, j], far_r.at[g, t, j], far_devices[j])

    def far_arrival(g, t, j):
        ref = x.at[g, t, held, y, far_blocks[j]]
        return remote(ref, ref, far_s.at[g, t, j], far_r.at[g, t, j], far_devices[j])

    def near_copy(g, t, n):
        ref = x.at[g, t, held, y, span(MESSAGES[n][2])]
        return remote(ref, ref, near_s.at[g, t, n], near_r.at[g, t, n], near_devices[n])

    def near_arrival(g, t, n):
        dz, dy, which, _ = MESSAGES[n]
        ref = x.at[g, t, (held - dz + NEAR) % NEAR, 1 - y if dy else y, span(which)]
        return remote(ref, ref, near_s.at[g, t, n], near_r.at[g, t, n], near_devices[n])

    def gather_far(g, t):
        for j in far_order:
            far_copy(g, t, j).start()

    def gather_near(g, t):
        for j in range(nq):
            far_arrival(g, t, j).wait_recv()
        for n in range(len(MESSAGES)):
            near_copy(g, t, n).start()

    def gather_end(g, t, out):
        def widen(mm, yy, which):
            piece = parts[which]
            count = (piece.stop - piece.start) * rb
            start = ((mm * 2 + yy) * nq + piece.start) * rb
            values = x[g, t, mm, yy, span(which)].astype(F32).reshape(count, LANES)
            xf[t, pl.ds(pl.multiple_of(start, 8), count), :] = values

        widen(held, y, "all")
        for n in ARRIVALS:
            dz, dy, which, _ = MESSAGES[n]
            near_arrival(g, t, n).wait_recv()
            widen((held - dz + NEAR) % NEAR, 1 - y if dy else y, which)
        for k in range(chunks):
            out[t, :, k * LANES:(k + 1) * LANES] = xf[t, pl.ds(k, rows, stride=chunks), :].astype(BF16)

    def gather_sent(g, t):
        for j in range(nq):
            far_copy(g, t, j).wait_send()
        for n in range(len(MESSAGES)):
            near_copy(g, t, n).wait_send()

    def sum_copy(g, t, i):
        j = peer(i)
        return remote(
            f_out.at[g, t, j], f_in.at[g, t, i], f_send.at[0, g, t, i], f_recv.at[0, g, t, i], feature_devices[i - 1]
        )

    def sum_start(g, t, values):
        for i in range(1, nf):
            j = peer(i)
            start = pl.multiple_of(j // 2 * fb, 8)
            f_out[g, t, j] = values[t, j % 2, pl.ds(start, fb), :].astype(BF16)
            sum_copy(g, t, i).start()

    def sum_end(g, t, values):
        acc = values[t, side, pl.ds(pl.multiple_of(feat // 2 * fb, 8), fb), :]
        for i in range(nf - 1, 0, -1):
            sum_copy(g, t, i).wait_recv()
            acc = acc + f_in[g, t, i].astype(F32)
        return acc

    def share_copy(t, i, mine):
        slot = codes.at[t, feat if mine else giver(i)]
        return remote(slot, slot, f_send.at[1, 0, t, i], f_recv.at[1, 0, t, i], feature_devices[i - 1])

    def share_start(t):
        for i in range(1, nf):
            share_copy(t, i, True).start()

    def share_end(t):
        for i in range(1, nf):
            share_copy(t, i, False).wait_recv()

    def give_copy(t, i):
        target = {"feature": peer(i), "latent": (z * 2 + y) * 2 + side}
        return remote(
            pre_own.at[t], pre_all.at[t, c, feat // 2], g_send.at[t, i], g_recv.at[t, c, feat // 2], target
        )

    def give_start(t):
        for i in range(1, nf):
            give_copy(t, i).start()

        @pl.when(side != c)
        def _():
            give_copy(t, 0).start()

        @pl.when(side == c)
        def _():
            pre_all[t, c, feat // 2] = pre_own[t]

    def give_end(t):
        for k in range(nf // 2):
            for cc in range(2):
                slot = pre_all.at[t, cc, k]
                arrival = remote(slot, slot, g_send.at[t, 0], g_recv.at[t, cc, k], other_core)

                @pl.when(jnp.logical_not((cc == c) & (2 * k + c == feat)))
                def _():
                    arrival.wait_recv()

    def give_sent(t):
        for i in range(1, nf):
            give_copy(t, i).wait_send()

        @pl.when(side != c)
        def _():
            give_copy(t, 0).wait_send()

    def sum_sent(g, t):
        for i in range(1, nf):
            sum_copy(g, t, i).wait_send()

    def local(t, mm, yy):
        start = (mm * 2 + yy) * group
        return blocks(xf[t, pl.ds(pl.multiple_of(start, 8), group), :])

    def blocks(value):
        return value.reshape(nq, rb, LANES)

    def rn_copy(t, n):
        dz, dy, which, slot = MESSAGES[n]
        mm = (held + dz + NEAR) % NEAR
        yy = 1 - y if dy else y
        return remote(
            near_out.at[t, mm, yy, span(which)], near_in.at[t, slot, span(which)],
            rn_s.at[t, n], rn_r.at[t, n], near_devices[n],
        )

    def reduce_near(t):
        for n, (dz, dy, which, _) in enumerate(MESSAGES):
            if which != "high":
                mm = (held + dz + NEAR) % NEAR
                yy = 1 - y if dy else y
                near_out[t, mm, yy] = local(t, mm, yy).astype(BF16)
            rn_copy(t, n).start()

    def rf_copy(t, j):
        return remote(far_out.at[t, j], far_in.at[t, j], rf_s.at[t, j], rf_r.at[t, j], far_devices[nq - 1 - j])

    def reduce_far(t):
        total[t] = local(t, held, y)
        for n in ARRIVALS:
            _, _, which, slot = MESSAGES[n]
            rn_copy(t, n).wait_recv()
            total[t, span(which)] = total[t, span(which)] + near_in[t, slot, span(which)].astype(F32)
        for j in far_order:
            far_out[t, j] = total[t, far_blocks[j]].astype(BF16)
            rf_copy(t, j).start()

    def reduce_end(t):
        acc = jnp.zeros((rb, LANES), F32)
        for j in reversed(far_order):
            rf_copy(t, j).wait_recv()
            acc = acc + far_in[t, j].astype(F32)
        own[1, t] = (acc - goal[t]).astype(BF16)
        total_rows[t] = acc

    def write_recon(t):
        for k in range(chunks):
            wide_rows[:, t, k * LANES:(k + 1) * LANES] = total_rows[t, pl.ds(k, own_rows, stride=chunks), :]

    def reduce_sent(t):
        for n in range(len(MESSAGES)):
            rn_copy(t, n).wait_send()
        for j in range(nq):
            rf_copy(t, j).wait_send()

    both = (0, 1)
    for t in both:
        gather_far(0, t)
    for copy in swaps:
        copy.start()
    for t in both:
        gather_near(0, t)
    load_enc.wait()
    for copy in swapped[:2]:
        copy.wait_recv()
    for t in both:
        gather_end(0, t, a_own)
        for cc in range(2):
            part[t, cc] = jnp.dot(a_own[t], enc[cc, t], preferred_element_type=F32)
        sum_start(0, t, part)
    store_act = [pltpu.make_async_copy(a_own.at[t], a_hbm.at[t, c], load_sem.at[2 + t]) for t in both]
    for t in both:
        store_act[t].start()
        act_copy(t).start()
        value = sum_end(0, t, part) + biases[side, t:t + 1, :]
        codes[t, feat] = (mask[t] * value).astype(BF16)
        share_start(t)
    load_dec.wait()
    swapped[2].wait_recv()

    def whole(t, cc):
        mine = [codes[t, 2 * k + cc].astype(F32) for k in range(nf // 2)]
        return jnp.concatenate(mine, axis=0)

    wide = 2 * LANES
    for t in both:
        share_end(t)
        terms = []
        for cc in range(2):
            if t == 0:
                terms.append((whole(0, cc).astype(BF16), cc, 0))
            else:
                lanes = slice(cc * latents, (cc + 1) * latents)
                terms.append(((whole(0, cc) * gate[:, lanes]).astype(BF16), cc, 1))
                terms.append((whole(1, cc).astype(BF16), cc, 2))
        for n in range(depth // wide):
            cols = slice(n * wide, (n + 1) * wide)
            value = sum(jnp.dot(code, dec[cc, p, :, cols], preferred_element_type=F32) for code, cc, p in terms)
            for k in range(2):
                xf[t, pl.ds(2 * n + k, rows, stride=chunks), :] = value[:, k * LANES:(k + 1) * LANES]
        reduce_near(t)
    for copy in swaps:
        copy.wait_send()
    for t in both:
        gather_sent(0, t)
        sum_sent(0, t)
        for i in range(1, nf):
            share_copy(t, i, True).wait_send()
    for t in both:
        reduce_far(t)
    for t in both:
        reduce_end(t)
        gather_far(1, t)
    for t in both:
        gather_near(1, t)
    for t in both:
        reduce_sent(t)
        write_recon(t)
    recon[...] = wide_rows[...].astype(BF16)
    store_recon = pltpu.make_async_copy(recon, recon_hbm, small_sem.at[0])
    store_recon.start()

    def gradient(t, cc, p):
        return lax.dot_general(err_own[t], dec[cc, p], across, preferred_element_type=F32)

    gather_end(1, 0, err_own)
    for cc in range(2):
        grad[0, cc] = gradient(0, cc, 0)
    gather_end(1, 1, err_own)
    for cc in range(2):
        grad[1, cc] = gradient(1, cc, 2)
    sum_start(1, 1, grad)
    for cc in range(2):
        grad[0, cc] = grad[0, cc] + gate[:, cc * latents:(cc + 1) * latents] * gradient(1, cc, 1)
    sum_start(1, 0, grad)
    for t in (1, 0):
        pre_own[t] = (mask[t] * sum_end(1, t, grad) * scale).astype(BF16)
        give_start(t)
    for t in both:
        gather_sent(1, t)
        sum_sent(1, t)
        store_act[t].wait()
        act_copy(t).wait_send()
        arrived = a_hbm.at[t, 1 - c]
        remote(arrived, arrived, swap_s.at[3 + t], swap_r.at[3 + t], other_core).wait_recv()
    store_pre = [pltpu.make_async_copy(pre_out.at[t], pre_hbm.at[t], small_sem.at[1 + t]) for t in both]
    for t in (1, 0):
        give_end(t)
        for cc in range(2):
            whole_rows = jnp.concatenate([pre_all[t, cc, k].astype(F32) for k in range(nf // 2)], axis=0)
            pre_out[t, cc] = whole_rows.astype(BF16)
        store_pre[t].start()
    store_recon.wait()
    for t in both:
        give_sent(t)
        store_pre[t].wait()


def body(nz, nf, activations, targets, enc_weight, enc_bias, dec_weight, top_blocks, pair_mask):
    own_rows, layers, depth = activations.shape
    all_rows = top_blocks.shape[0]
    rows = all_rows // 2
    latents = enc_weight.shape[2]
    chunks = depth // LANES
    rb = own_rows * chunks
    fb = all_rows // nf
    nq = nz // NEAR
    hbm = pl.BlockSpec(memory_space=pltpu.HBM)
    dma = pltpu.SemaphoreType.DMA
    bf, f32 = (lambda *s: pltpu.VMEM(s, BF16)), (lambda *s: pltpu.VMEM(s, F32))
    count = len(MESSAGES)
    recon, a_all, pre_grad = pl.pallas_call(
        functools.partial(kernel, nz, nf, 1.0 / math.sqrt(all_rows)),
        out_shape=(
            jax.ShapeDtypeStruct(activations.shape, BF16),
            jax.ShapeDtypeStruct((layers, 2, rows, depth), BF16),
            jax.ShapeDtypeStruct((layers, 2, rows, latents), BF16),
        ),
        in_specs=[hbm] * 7,
        out_specs=(hbm, hbm, hbm),
        scratch_shapes=[
            bf(*activations.shape),
            bf(*targets.shape),
            f32(*enc_bias.shape),
            pltpu.VMEM((layers, top_blocks.shape[2], all_rows), jnp.int32),
            pltpu.VMEM(pair_mask.shape, jnp.int32),
            bf(*activations.shape),
            bf(layers, 2, rows, latents),
            bf(layers, rows, depth),
            bf(2, *enc_weight.shape),
            bf(2, *dec_weight.shape),
            f32(2, *enc_bias.shape),
            bf(2, layers, rb, LANES),
            f32(layers, rb, LANES),
            f32(own_rows, layers, depth),
            f32(layers, fb, latents),
            f32(1, 2 * latents),
            bf(2, layers, NEAR, 2, nq, rb, LANES),
            f32(layers, rows * chunks, LANES),
            bf(layers, rows, depth),
            f32(layers, 2, rows, latents),
            f32(layers, 2, rows, latents),
            bf(2, layers, nf, fb, latents),
            bf(2, layers, nf, fb, latents),
            bf(layers, nf, fb, latents),
            bf(layers, fb, latents),
            bf(layers, 2, nf // 2, fb, latents),
            bf(layers, NEAR, 2, nq, rb, LANES),
            bf(layers, SLOTS, nq, rb, LANES),
            f32(layers, nq, rb, LANES),
            f32(layers, rb, LANES),
            bf(layers, nq, rb, LANES),
            bf(layers, nq, rb, LANES),
            dma((4,)),
            dma((5,)),
            dma((5,)),
            dma((5,)),
            dma((2, layers, nq)),
            dma((2, layers, nq)),
            dma((2, layers, count)),
            dma((2, layers, count)),
            dma((2, 2, layers, nf)),
            dma((2, 2, layers, nf)),
            dma((layers, nf)),
            dma((layers, 2, nf // 2)),
            dma((layers, count)),
            dma((layers, count)),
            dma((layers, nq)),
            dma((layers, nq)),
        ],
        compiler_params=pltpu.CompilerParams(
            collective_id=0, has_side_effects=True, vmem_limit_bytes=63 * 2**20
        ),
    )(
        activations, targets, enc_weight, enc_bias, dec_weight, top_blocks.transpose(1, 2, 0), pair_mask,
    )
    enc_grad = jnp.einsum(
        "lrd,lrf->ldf",
        a_all.reshape(layers, all_rows, depth),
        pre_grad.reshape(layers, all_rows, latents),
        preferred_element_type=F32,
    )
    return recon, enc_grad


def solution(mesh):
    in_specs = (
        P("latent", None, "feature"),
        P("latent", None, "feature"),
        P(None, "feature", "latent"),
        P(None, "latent"),
        P(None, "latent", "feature"),
        P(),
        P(),
    )
    out_specs = (P("latent", None, "feature"), P(None, "feature", "latent"))
    step = functools.partial(body, mesh.shape["latent"] // 4, mesh.shape["feature"])
    return jax.shard_map(step, mesh=mesh, in_specs=in_specs, out_specs=out_specs, check_vma=False)
```
